128 devices in a mesh: row: 8 (over x, core), col: 16 (over z, y).
Axes of the slice: x: 4, y: 4, z: 4, core: 2. Of those that a mesh axis runs over, the one named last changes fastest.
Arguments:
- reflectance: bfloat16 [4, 65536, 128], P(None, ('row', 'col')), may hold values from 0.049804688 to 0.59765625
- kernel_id: int32 [65536], P(('row', 'col')), may hold values from 0 to 7
- dest_device: int32 [65536, 1], P(('row', 'col')), may hold values from 0 to 127; in each aligned block of 512 rows (0 to 511, 512 to 1023, ...) at most 8 rows name the same one
- dest_block: int32 [65536], P(('row', 'col')), may hold values from 0 to 511
- regrid_weight: bfloat16 [8, 128, 128], replicated, may hold values from 0 to 0.82, as said below
- depth0: float32 [512, 16384], P('row', 'col'), may hold values from 0.01 to 3, as said below
- terrain: float32 [512, 16384], P('row', 'col'), may hold values from -0.6 to 0.6
- rain: float32 [512, 16384], P('row', 'col'), may hold values from 0.01 to 0.1
- burn_mask: int32 [512, 16384], P('row', 'col'), may hold values 0 or 1
- land_class: int32 [512, 16384], P('row', 'col'), may hold values from 0 to 15
- infil_table: float32 [16], replicated, may hold values from 0.01 to 0.1
- rough_table: float32 [16], replicated, may hold values from 0.02 to 0.2
Outputs:
- depth: float32 [512, 16384], P('row', 'col')
- east_flow: float32 [512, 16384], P('row', 'col')
- north_flow: float32 [512, 16384], P('row', 'col')
The draws below stay inside these ranges and needn't reach their ends.
Inputs may be any that keep to these rules, and one draw needn't show every extreme that they name: `dest_device`: the sensor blocks of one device name each destination device at most 8 times, a bound that some block reaches. `regrid_weight`: Nonnegative; the diagonal of each block exceeds 0.4. `depth0`: the largest depth differs from draw to draw.
All inputs are finite; a program needn't handle non-finite values. No bound on the sum of `burn_mask` on one device may be relied on, other than what follows from the above.
Results may differ from the reference program's by a relative error of at most 0.0003.
Values sent between devices are 32-bit elements; how exact they have to be, the bound alone decides.
A program may use at most 64 MiB of HBM per device.

```python
import math
import jax
import jax.numpy as jnp
import numpy as np

TR = 64
TC = 1024
BLOCK = 128
NK = 8
NLC = 16
ITERS = 6
NB = 512
CAP = 8
SB = 65536
NR = 512
NC = 16384
N_ROW = 8
N_COL = 16
DEVICES = 128


def draw_regrid_weight(key, part):
    first = jax.random.fold_in(key, 11)
    second = jax.random.fold_in(key, 12)
    diagonal = jax.random.uniform(first, (NK, BLOCK, 1), jnp.float32, 0.4, 0.8)
    spread = jax.random.uniform(second, (NK, BLOCK, BLOCK), jnp.float32, 0.0, 1.2) / 128.0
    rows = jnp.arange(BLOCK)[:, None]
    cols = jnp.arange(BLOCK)[None, :]
    on_diag = (rows == cols)[None, :, :]
    return jnp.where(on_diag, diagonal + spread, spread).astype(jnp.bfloat16)


def draw_depth0(key, part):
    first = jax.random.fold_in(key, 21)
    second = jax.random.fold_in(key, 22)
    ramp = 1.0 + 2.0 * (jnp.arange(NR, dtype=jnp.float32) / NR)[:, None]
    factor = jax.random.uniform(second, (), jnp.float32, 0.5, 1.0)
    base = jnp.exp(jax.random.uniform(first, (NR, NC), jnp.float32, jnp.log(0.01), 0.0))
    return jnp.clip(base * ramp * factor, 0.01, 3.0)


def set_ends(entries, rng, least, high):
    spot = [jax.random.randint(jax.random.fold_in(rng, axis), (), 0, length) for axis, length in enumerate(entries.shape)]
    main_axis = entries.shape.index(max(entries.shape))
    beside = spot[:main_axis] + [(spot[main_axis] + 1) % entries.shape[main_axis]] + spot[main_axis + 1:]
    return entries.at[tuple(spot)].set(least).at[tuple(beside)].set(high)


def block_levels(stream_key, shape, cuts, least, high):
    level, own = 1.0, jax.random.fold_in(stream_key, 6)
    for dim, parts in cuts:
        steps = jnp.exp(jax.random.uniform(jax.random.fold_in(own, dim), (parts,), jnp.float32, least / len(cuts), high / len(cuts)))
        level = level * jnp.repeat(steps, shape[dim] // parts).reshape([-1 if axis == dim else 1 for axis in range(len(shape))])
    return level


def shared_out(own_key, own, number, rows, amount, top, most, slope):
    ranking = jax.random.permutation(own_key, amount)
    packed, usual = load_shares(amount, rows * top, most, slope, True), load_shares(amount, rows * top, most, slope, False)
    places = jnp.arange(amount)

    def named(tallies, turn):
        used = int((tallies > 0).sum())
        fixed = max(1, used // 4)
        shifted = fixed + (places - fixed + turn * (used - fixed)) % max(1, amount - fixed)
        return jnp.zeros((amount,), jnp.int32).at[ranking[jnp.where(places < fixed, places, shifted)]].set(jnp.asarray(tallies, jnp.int32))

    tallies = jnp.where(number % 4 == 0, named(packed, number // 4), named(usual, number - number // 4 - 1))
    mixed = jax.random.permutation(jax.random.fold_in(own, 3), amount)
    source_of, receiver = mixed[0:amount // 2 * 2:2], mixed[1:amount // 2 * 2:2]
    slack = jnp.minimum(tallies[source_of] - 1, most - tallies[receiver]) // 2
    slack = jnp.where((source_of == ranking[0]) | (receiver == ranking[0]) | (tallies[receiver] == 0), 0, jnp.maximum(slack, 0))
    shifted = jax.random.randint(jax.random.fold_in(own, 4), (amount // 2,), 0, 1 << 20) % (slack + 1)
    tallies = tallies.at[source_of].add(-shifted).at[receiver].add(shifted)
    labels = jnp.searchsorted(jnp.cumsum(tallies), jnp.arange(rows * top), side="right").astype(jnp.int32)
    grid = labels.reshape(top, rows).T
    grid = grid[jax.random.permutation(jax.random.fold_in(own, 1), rows)]
    turn = jax.random.randint(jax.random.fold_in(own, 2), (rows, 1), 0, top)
    return jnp.take_along_axis(grid, (jnp.arange(top)[None, :] + turn) % top, axis=1)


def load_shares(count, total, most, slope, full):
    weights = [(1 << 20) // math.isqrt(standing ** slope) + 1 for standing in range(1, count + 1)]
    largest = most if full else min(most, max(-(-total // count), total * weights[0] // sum(weights)))
    least = 1 if total - largest >= count - 1 else 0
    counts, spare = [largest] + [least] * (count - 1), total - largest - least * (count - 1)
    while spare > 0:
        candidates = [i for i in range(1, count) if counts[i] < largest] or [i for i in range(1, count) if counts[i] < most]
        pool, remaining = sum([weights[i] for i in candidates]), spare
        for i in candidates:
            addition = min(most - counts[i], max(1, remaining * weights[i] // pool), spare)
            counts[i] = counts[i] + addition
            spare = spare - addition
    return np.array(counts)


def scatter_about(key, dims, scale, most, split=(), kind=jnp.bfloat16):
    values = scale * jax.random.normal(key, dims, jnp.float32)
    if split:
        values = values * block_levels(key, dims, split, -0.22, 0.18)
    return jnp.clip(values, -most, most).astype(kind)


def setup_inputs(seed: int = 0) -> dict:
    splits = jax.random.split(jax.random.key(seed), 13)
    reflectance = jnp.clip(0.049804688 + 0.54785156 * jax.random.uniform(splits[0], (4, SB, BLOCK), jnp.float32) ** block_levels(splits[0], (4, SB, BLOCK), ((1, 128),), -0.2, 0.2), 0.049804688, 0.59765625).astype(jnp.bfloat16)
    kernel_id = set_ends(jax.random.randint(splits[1], (SB,), 0, NK), jax.random.fold_in(splits[1], 1), 0, NK - 1).astype(jnp.int32)
    dest_device_keys = jax.random.split(jax.random.fold_in(splits[2], 1), SB // NB)
    dest_device_turns = jax.random.permutation(jax.random.fold_in(splits[2], 3), SB // NB)
    dest_device = jax.vmap(lambda own, number: shared_out(jax.random.fold_in(splits[2], 2), own, number, NB, DEVICES, 1, CAP, 2))(dest_device_keys, dest_device_turns).reshape((SB, 1))
    dest_block = set_ends(jax.random.randint(splits[3], (SB,), 0, NB), jax.random.fold_in(splits[3], 1), 0, NB - 1).astype(jnp.int32)
    regrid_weight = draw_regrid_weight(jax.random.fold_in(splits[12], 71), 0)
    depth0 = draw_depth0(jax.random.fold_in(splits[12], 71), 0)
    terrain = scatter_about(splits[6], (NR, NC), 0.1, 0.6, ((0, 8), (1, 16)), jnp.float32)
    rain = jnp.clip(jnp.exp(math.log(0.1) - 2.3025851 * jax.random.uniform(splits[7], (NR, NC), jnp.float32) ** block_levels(splits[7], (NR, NC), ((0, 8), (1, 16)), -0.2, 0.2)), 0.01, 0.1)
    burn_mask = set_ends((jax.random.randint(splits[8], (NR, NC), 0, 2) < 1).astype(jnp.int32), jax.random.fold_in(splits[8], 1), 0, 1)
    land_class = set_ends(jax.random.randint(splits[9], (NR, NC), 0, NLC), jax.random.fold_in(splits[9], 1), 0, NLC - 1).astype(jnp.int32)
    infil_table = jnp.clip(jnp.exp(jax.random.uniform(splits[10], (NLC,), jnp.float32, math.log(0.01), math.log(0.1))), 0.01, 0.1)
    rough_table = jnp.clip(jnp.exp(jax.random.uniform(splits[11], (NLC,), jnp.float32, math.log(0.02), math.log(0.2))), 0.02, 0.2)
    return dict(reflectance=reflectance, kernel_id=kernel_id, dest_device=dest_device, dest_block=dest_block, regrid_weight=regrid_weight, depth0=depth0, terrain=terrain, rain=rain, burn_mask=burn_mask, land_class=land_class, infil_table=infil_table, rough_table=rough_table)


GRAVITY = 9.81
CELL_SIZE = 10.0
COURANT = 0.4
DEPTH_FLOOR = 0.05
BURN_LOSS = 1.5
BURN_SMOOTH = 0.5

def ratio(nir, swir):
    return (nir - swir) / (nir + swir)

def lookup(table, classes):
    result = jnp.zeros(classes.shape, jnp.float32)
    for entry in range(table.shape[0]):
        result = result + jnp.where(classes == entry, table[entry], jnp.float32(0.0))
    return result

def wave_speed(state):
    floored = jnp.maximum(state[0], DEPTH_FLOOR)
    celerity = jnp.sqrt(GRAVITY * jnp.maximum(state[0], 0.0))
    return jnp.maximum(jnp.abs(state[1] / floored), jnp.abs(state[2] / floored)) + celerity

def advance(padded, relief, roughness, capacity_in, rainfall, time_step):
    depth = padded[0]
    east = padded[1]
    north = padded[2]
    floored = jnp.maximum(depth, DEPTH_FLOOR)
    east_speed = east / floored
    north_speed = north / floored
    celerity = jnp.sqrt(GRAVITY * jnp.maximum(depth, 0.0))
    pressure = 0.5 * GRAVITY * depth * depth
    flux_east = jnp.stack([east, east * east_speed + pressure, east * north_speed])
    flux_north = jnp.stack([north, north * east_speed, north * north_speed + pressure])
    reach_east = jnp.abs(east_speed) + celerity
    reach_north = jnp.abs(north_speed) + celerity
    face_reach = jnp.maximum(reach_east[:, :-1], reach_east[:, 1:])
    face_east = 0.5 * (flux_east[:, :, :-1] + flux_east[:, :, 1:]) - 0.5 * face_reach * (padded[:, :, 1:] - padded[:, :, :-1])
    row_reach = jnp.maximum(reach_north[:-1], reach_north[1:])
    face_north = 0.5 * (flux_north[:, :-1] + flux_north[:, 1:]) - 0.5 * row_reach * (padded[:, 1:] - padded[:, :-1])
    change = (face_east[:, 1:-1, 1:] - face_east[:, 1:-1, :-1] + face_north[:, 1:, 1:-1] - face_north[:, :-1, 1:-1]) / CELL_SIZE
    old = padded[:, 1:-1, 1:-1]
    old_depth = depth[1:-1, 1:-1]
    slope_east = (relief[1:-1, 2:] - relief[1:-1, :-2]) / (2.0 * CELL_SIZE)
    slope_north = (relief[2:, 1:-1] - relief[:-2, 1:-1]) / (2.0 * CELL_SIZE)
    wetted = old[0] - time_step * change[0] + time_step * rainfall
    wetted = wetted - jnp.minimum(time_step * capacity_in, wetted)
    moved_east = old[1] - time_step * change[1] - time_step * GRAVITY * old_depth * slope_east
    moved_north = old[2] - time_step * change[2] - time_step * GRAVITY * old_depth * slope_north
    inner_floor = floored[1:-1, 1:-1]
    magnitude = jnp.sqrt(east_speed[1:-1, 1:-1] ** 2 + north_speed[1:-1, 1:-1] ** 2)
    drag = 1.0 + time_step * GRAVITY * roughness * roughness * magnitude / inner_floor ** (4.0 / 3.0)
    return jnp.stack([wetted, moved_east / drag, moved_north / drag])

def reference(reflectance, kernel_id, dest_device, dest_block, regrid_weight, depth0, terrain, rain, burn_mask, land_class, infil_table, rough_table):
    bands = reflectance.astype(jnp.float32)
    burn_index = (ratio(bands[0], bands[1]) - ratio(bands[2], bands[3])).astype(jnp.bfloat16)
    regridded = jnp.zeros(burn_index.shape, jnp.float32)
    for kernel in range(regrid_weight.shape[0]):
        product = jnp.dot(burn_index, regrid_weight[kernel], preferred_element_type=jnp.float32)
        regridded = jnp.where((kernel_id == kernel)[:, None], product, regridded)
    target = (dest_device[:, 0] * NB + dest_block).astype(jnp.int32)
    gathered = jnp.zeros((DEVICES * NB, burn_index.shape[1]), jnp.float32).at[target].add(regridded)
    severity = gathered.reshape(N_ROW, N_COL, TR, TC).transpose(0, 2, 1, 3).reshape(TR * N_ROW, TC * N_COL)
    burned = burn_mask.astype(jnp.float32)
    infiltration = lookup(infil_table, land_class) * jnp.exp(-BURN_LOSS * burned * jnp.maximum(severity, 0.0))
    roughness = lookup(rough_table, land_class) * (1.0 - BURN_SMOOTH * burned)
    zeros_field = jnp.zeros(depth0.shape, jnp.float32)
    state = jnp.stack([depth0, zeros_field, zeros_field])
    relief = jnp.pad(terrain, 1)
    for iteration in range(ITERS):
        time_step = COURANT * CELL_SIZE / jnp.max(wave_speed(state))
        padded = jnp.pad(state, ((0, 0), (1, 1), (1, 1)))
        state = advance(padded, relief, roughness, infiltration, rain, time_step)
    return (state[0], state[1], state[2])
```

```python
import jax
import jax.numpy as jnp
from jax import lax
from jax.experimental import pallas as pl
from jax.experimental.pallas import tpu as pltpu
from jax.sharding import PartitionSpec as P

ITERS = 6
GRAVITY = 9.81
CELL_SIZE = 10.0
COURANT = 0.4
DEPTH_FLOOR = 0.05
BURN_LOSS = 1.5
BURN_SMOOTH = 0.5

LOGICAL = pl.DeviceIdType.LOGICAL
F32 = jnp.float32
BF16 = jnp.bfloat16

HOPS = (0, 1, 2, 1)
OFFSETS = sorted(
    [
        (x, core, z, y)
        for x in range(4)
        for core in range(2)
        for z in range(4)
        for y in range(4)
        if (x, core, z, y) != (0, 0, 0, 0)
    ],
    key=lambda o: (-(HOPS[o[0]] + HOPS[o[2]] + HOPS[o[3]]), -o[1]),
)
PEERS = len(OFFSETS)
DEVICES = PEERS + 1

CG = 8
TR = 64
PADR = TR + 16
TOP = 8


def approx_recip(value):
    guess = pl.reciprocal(value, approx=True)
    return guess * (2.0 - value * guess)


def root(value):
    safe = jnp.maximum(value, 1e-30)
    return safe * lax.rsqrt(safe)


def lanes(shape):
    return lax.broadcasted_iota(jnp.int32, shape, len(shape) - 1)


def nt_dot(a, b):
    return lax.dot_general(a, b, (((1,), (1,)), ((), ())), preferred_element_type=F32)


def kernel(
    refl_hbm, kid_hbm, dest_hbm, block_hbm, weight_hbm, depth_hbm, terrain_hbm, rain_hbm, burn_hbm, land_hbm,
    infil_tab, rough_tab,
    depth_out, east_out, north_out,
    refl, kid, dest, block, weight, rain, burn, land,
    state, bed, derived, drag_k, rate, infil, rough2, slope_e, slope_n,
    burn_index, outgoing, incoming, label_tile, label_out, label_in, label_q,
    max_out, max_in, row_out, row_in, col_out, col_in,
    in_sem, bulk_sem, halo_send, halo_recv, max_send, max_recv, out_sem,
):
    my_row, my_col = lax.axis_index("row"), lax.axis_index("col")
    rows_n, cols_n = 8, 16
    me = my_row * cols_n + my_col
    x, core, z, y = my_row // 2, lax.rem(my_row, 2), my_col // 4, lax.rem(my_col, 4)
    xs = [lax.rem(x + d, 4) * 32 for d in range(4)]
    cores = [lax.rem(core + d, 2) * 16 for d in range(2)]
    zs = [lax.rem(z + d, 4) * 4 for d in range(4)]
    ys = [lax.rem(y + d, 4) for d in range(4)]
    xc = [[a + b for b in cores] for a in xs]
    zy = [[a + b for b in ys] for a in zs]

    def target(o):
        return xc[o[0]][o[1]] + zy[o[2]][o[3]]

    south_dev = lax.rem(my_row + 1, rows_n) * cols_n + my_col
    north_dev = lax.rem(my_row + rows_n - 1, rows_n) * cols_n + my_col
    east_dev = my_row * cols_n + lax.rem(my_col + 1, cols_n)
    west_dev = my_row * cols_n + lax.rem(my_col + cols_n - 1, cols_n)

    def grid_copies(src, dst_of, sem):
        return [
            pltpu.make_async_copy(src.at[:, pl.ds(c * 128, 128)], dst_of(c), sem) for c in range(CG)
        ]

    loads = {
        "dest": [pltpu.make_async_copy(dest_hbm, dest, in_sem.at[0])],
        "kid": [pltpu.make_async_copy(kid_hbm, kid, in_sem.at[1])],
        "block": [pltpu.make_async_copy(block_hbm, block, in_sem.at[2])],
        "refl": [pltpu.make_async_copy(refl_hbm, refl, in_sem.at[3])],
        "weight": [pltpu.make_async_copy(weight_hbm, weight, in_sem.at[4])],
    }
    tile_rows = pl.ds(TOP, TR)
    grids = {
        "depth": (depth_hbm, lambda c: state.at[0, c + 1, tile_rows], 5),
        "terrain": (terrain_hbm, lambda c: bed.at[c + 1, tile_rows], 6),
        "land": (land_hbm, lambda c: land.at[c], 7),
        "burn": (burn_hbm, lambda c: burn.at[c], 8),
        "rain": (rain_hbm, lambda c: rain.at[c], 9),
    }
    for name, (src, dst_of, slot) in grids.items():
        loads[name] = [
            pltpu.make_async_copy(src.at[:, pl.ds(c * 128, 128)], dst_of(c), in_sem.at[slot + 5 * c])
            for c in range(CG)
        ]
    for name in ("dest", "block", "kid", "refl", "weight", "depth", "terrain", "land", "burn", "rain"):
        for copy in loads[name]:
            copy.start()

    def arrive(name):
        for copy in loads[name]:
            copy.wait()

    barrier = pltpu.get_barrier_semaphore()
    for o in OFFSETS:
        pl.semaphore_signal(barrier, inc=1, device_id=target(o), device_id_type=LOGICAL)

    edge = jnp.zeros((8, 128), F32)
    wide = jnp.zeros((PADR, 128), F32)

    def clear(c, _):
        state[1, c] = wide
        state[2, c] = wide
        for ref in (state.at[0], bed):
            ref[c, pl.ds(0, 8), :] = edge
            ref[c, pl.ds(TOP + TR, 8), :] = edge
        return 0

    lax.fori_loop(0, CG + 2, clear, 0)
    for c in (0, CG + 1):
        state[0, c] = wide
        bed[c] = wide

    arrive("dest")
    arrive("block")
    arrive("kid")
    dest_row = dest[...]
    blocks = dest_row.shape[1]
    member = lax.broadcasted_iota(jnp.int32, (DEVICES, blocks), 0) == dest_row
    member_f = jnp.where(member, 1.0, 0.0).astype(F32)
    member_b = member_f.astype(BF16)
    upper = jnp.where(
        lax.broadcasted_iota(jnp.int32, (blocks, blocks), 0) <= lanes((blocks, blocks)), 1.0, 0.0
    ).astype(BF16)
    counts = jnp.dot(member_b, upper, preferred_element_type=F32)
    rank = jnp.sum(member_f * counts, axis=0, keepdims=True) - 1.0
    position = dest_row.astype(F32) * 8.0 + rank

    block_row = block[...]
    high = (block_row // 16).astype(F32)
    low = lax.rem(block_row, 16).astype(F32)
    line = lax.broadcasted_iota(jnp.int32, (128, blocks), 0)
    by_rank = jnp.where(line.astype(F32) == rank, high, jnp.where(line.astype(F32) - 8.0 == rank, low, 0.0))
    label_tile[...] = nt_dot(member_b, by_rank.astype(BF16))

    arrive("refl")

    def index_chunk(i, _):
        rows = pl.ds(pl.multiple_of(i * 64, 64), 64)
        bands = [refl[b, rows, :].astype(F32) for b in range(4)]
        pre = (bands[0] - bands[1]) / (bands[0] + bands[1])
        post = (bands[2] - bands[3]) / (bands[2] + bands[3])
        burn_index[rows, :] = (pre - post).astype(BF16)
        return 0

    lax.fori_loop(0, blocks // 64, index_chunk, 0)

    arrive("weight")
    kid_lines = jnp.broadcast_to(kid[...].astype(F32), (128, blocks)).astype(BF16)
    stacked = weight[...].reshape(8 * 128, 128)

    def send_chunk(i, _):
        want = (lax.broadcasted_iota(jnp.int32, (128, blocks), 0) + i * 128).astype(F32)
        pick = jnp.where(want == position, 1.0, 0.0).astype(BF16)
        rows = jnp.dot(pick, burn_index[...], preferred_element_type=F32)
        which = nt_dot(pick, kid_lines)
        spread = jnp.concatenate(
            [jnp.where(which == float(k), rows, 0.0).astype(BF16) for k in range(8)], axis=1
        )
        result = jnp.dot(spread, stacked, preferred_element_type=F32)
        outgoing[pl.ds(pl.multiple_of(i * 16, 16), 16)] = result.reshape(16, 8, 128)
        return 0

    lax.fori_loop(0, DEVICES * 8 // 128, send_chunk, 0)

    arrive("depth")

    def deepest(c, best):
        return jnp.maximum(best, jnp.max(state[0, c + 1, tile_rows, :].reshape(8, 8, 128), axis=0))

    best = lax.fori_loop(0, CG, deepest, jnp.zeros((8, 128), F32))
    best = jnp.max(jnp.max(best, axis=0, keepdims=True), axis=1, keepdims=True)
    lane_row = lanes((1, 128))

    def label_line(i, _):
        label_out[i] = jnp.where(lane_row < 16, label_tile[pl.ds(i, 1), :], best)
        return 0

    lax.fori_loop(0, DEVICES, label_line, 0)

    lane_tile = lanes((8, 128))

    def pack(fields, it):
        for f, ref in enumerate(fields):
            for c in range(CG):
                row_out[it, 0, f * CG + c, :] = ref[c + 1, TOP, :]
                row_out[it, 1, f * CG + c, :] = ref[c + 1, TOP + TR - 1, :]
        first = jnp.zeros((8, 128), F32)
        last = jnp.zeros((8, 128), F32)
        for f, ref in enumerate(fields):
            for r in range(8):
                spot = r * 4 + f
                rows = pl.ds(TOP + r * 8, 8)
                first = jnp.where(lane_tile == spot, pltpu.roll(ref[1, rows, :], spot, 1), first)
                last = jnp.where(lane_tile == spot, pltpu.roll(ref[CG, rows, :], spot + 1, 1), last)
        col_out[it, 0] = first
        col_out[it, 1] = last

    def halo_copies(it):
        moves = (
            (row_out, row_in, 0, 1, north_dev, 0),
            (row_out, row_in, 1, 0, south_dev, 1),
            (col_out, col_in, 0, 1, west_dev, 2),
            (col_out, col_in, 1, 0, east_dev, 3),
        )
        return [
            pltpu.make_async_remote_copy(
                src_ref=src.at[it, a],
                dst_ref=dst.at[it, b],
                send_sem=halo_send.at[it, s],
                recv_sem=halo_recv.at[it, s],
                device_id=dev,
                device_id_type=LOGICAL,
            )
            for src, dst, a, b, dev, s in moves
        ]

    keep = (
        jnp.where(my_row > 0, 1.0, 0.0).astype(F32),
        jnp.where(my_row < rows_n - 1, 1.0, 0.0).astype(F32),
        jnp.where(my_col > 0, 1.0, 0.0).astype(F32),
        jnp.where(my_col < cols_n - 1, 1.0, 0.0).astype(F32),
    )

    def unpack(fields, it):
        for f, ref in enumerate(fields):
            for c in range(CG):
                ref[c + 1, TOP - 1, :] = row_in[it, 0, f * CG + c, :] * keep[0]
                ref[c + 1, TOP + TR, :] = row_in[it, 1, f * CG + c, :] * keep[1]
        west = col_in[it, 0] * keep[2]
        east = col_in[it, 1] * keep[3]
        for f, ref in enumerate(fields):
            for r in range(8):
                spot = r * 4 + f
                rows = pl.ds(TOP + r * 8, 8)
                ref[0, rows, :] = pltpu.roll(west, 127 - spot, 1)
                ref[CG + 1, rows, :] = pltpu.roll(east, (128 - spot) % 128, 1)

    state_refs = [state.at[f] for f in range(3)]
    arrive("terrain")
    pack([state.at[0], bed], 0)

    pl.semaphore_wait(barrier, PEERS)

    def data_copy(k, o):
        there = target(o)
        return pltpu.make_async_remote_copy(
            src_ref=outgoing.at[there],
            dst_ref=incoming.at[k],
            send_sem=bulk_sem.at[0],
            recv_sem=bulk_sem.at[1],
            device_id=there,
            device_id_type=LOGICAL,
        )

    def label_copy(k, o):
        there = target(o)
        return pltpu.make_async_remote_copy(
            src_ref=label_out.at[there],
            dst_ref=label_in.at[k],
            send_sem=bulk_sem.at[2],
            recv_sem=bulk_sem.at[3],
            device_id=there,
            device_id_type=LOGICAL,
        )

    for copy in halo_copies(0):
        copy.start()
    for k, o in enumerate(OFFSETS):
        data_copy(k, o).start()
        for j in (2 * k, 2 * k + 1):
            if j < PEERS:
                label_copy(j, OFFSETS[j]).start()
    incoming[PEERS] = outgoing[me]
    label_in[PEERS] = label_out[me]

    arrive("land")
    arrive("burn")
    arrive("rain")

    def classes(c, _):
        for r in range(8):
            rows = pl.ds(r * 8, 8)
            kind = land[c, rows, :]
            burned = burn[c, rows, :].astype(F32)
            soak = jnp.full((8, 128), infil_tab[0], F32)
            manning = jnp.full((8, 128), rough_tab[0], F32)
            for entry in range(1, 16):
                hit = kind == entry
                soak = jnp.where(hit, infil_tab[entry], soak)
                manning = jnp.where(hit, rough_tab[entry], manning)
            manning = manning * (1.0 - BURN_SMOOTH * burned)
            infil[c, rows, :] = soak
            rough2[c, rows, :] = GRAVITY * manning * manning
        return 0

    lax.fori_loop(0, CG, classes, 0)

    def west_of(ref, c, rows):
        return pltpu.roll(jnp.where(lane_tile == 127, ref[c, rows, :], ref[c + 1, rows, :]), 1, 1)

    def east_of(ref, c, rows):
        return pltpu.roll(jnp.where(lane_tile == 0, ref[c + 2, rows, :], ref[c + 1, rows, :]), 127, 1)

    def derive(c, rows, r):
        depth, east, north = state[0, c, rows, :], state[1, c, rows, :], state[2, c, rows, :]
        floored = jnp.maximum(depth, DEPTH_FLOOR)
        inverse = approx_recip(floored)
        east_speed, north_speed = east * inverse, north * inverse
        celerity = root(GRAVITY * depth)
        pressure = (0.5 * GRAVITY) * depth * depth
        derived[0, c, rows, :] = east * east_speed + pressure
        derived[1, c, rows, :] = east * north_speed
        derived[2, c, rows, :] = north * north_speed + pressure
        derived[3, c, rows, :] = jnp.abs(east_speed) + celerity
        derived[4, c, rows, :] = jnp.abs(north_speed) + celerity
        if r is not None:
            inner = pl.ds(r * 8, 8)
            magnitude = root(east_speed * east_speed + north_speed * north_speed)
            power = jnp.exp((-4.0 / 3.0) * jnp.log(floored))
            drag_k[c - 1, inner, :] = rough2[c - 1, inner, :] * magnitude * power

    def derive_inside():
        def group(c, _):
            for r in range(8):
                derive(c + 1, pl.ds(TOP + r * 8, 8), r)
            return 0

        lax.fori_loop(0, CG, group, 0)

    def derive_edges():
        def group(c, _):
            derive(c + 1, pl.ds(0, 8), None)
            derive(c + 1, pl.ds(TOP + TR, 8), None)
            return 0

        lax.fori_loop(0, CG, group, 0)
        for c in (0, CG + 1):
            for r in range(8):
                derive(c, pl.ds(TOP + r * 8, 8), None)

    def flux():
        def group(c, _):
            for r in range(8):
                inner = pl.ds(r * 8, 8)
                rows, above, below = (pl.ds(TOP + r * 8 + s, 8) for s in (0, -1, 1))
                q = [state[f, c + 1, rows, :] for f in range(3)]
                flux_e = [q[1], derived[0, c + 1, rows, :], derived[1, c + 1, rows, :]]
                total = []
                refs = [state.at[0], state.at[1], state.at[2], derived.at[0], derived.at[1], derived.at[3]]
                d_w, e_w, n_w, a_w, b_w, reach_w = [west_of(ref, c, rows) for ref in refs]
                d_e, e_e, n_e, a_e, b_e, reach_e = [east_of(ref, c, rows) for ref in refs]
                reach = derived[3, c + 1, rows, :]
                face_w, face_e = jnp.maximum(reach, reach_w), jnp.maximum(reach, reach_e)
                for mid, q_w, q_e, f_w, f_e in (
                    (q[0], d_w, d_e, e_w, e_e),
                    (q[1], e_w, e_e, a_w, a_e),
                    (q[2], n_w, n_e, b_w, b_e),
                ):
                    total.append((f_e - f_w) - face_e * (q_e - mid) + face_w * (mid - q_w))
                q_n = [state[f, c + 1, above, :] for f in range(3)]
                q_s = [state[f, c + 1, below, :] for f in range(3)]
                reach = derived[4, c + 1, rows, :]
                face_n = jnp.maximum(reach, derived[4, c + 1, above, :])
                face_s = jnp.maximum(reach, derived[4, c + 1, below, :])
                g_n = [q_n[2], derived[1, c + 1, above, :], derived[2, c + 1, above, :]]
                g_s = [q_s[2], derived[1, c + 1, below, :], derived[2, c + 1, below, :]]
                for f in range(3):
                    total[f] = total[f] + (
                        (g_s[f] - g_n[f]) - face_s * (q_s[f] - q[f]) + face_n * (q[f] - q_n[f])
                    )
                scale = 0.5 / CELL_SIZE
                rate[0, c, inner, :] = rain[c, inner, :] - scale * total[0]
                rate[1, c, inner, :] = -scale * total[1] - q[0] * slope_e[c, inner, :]
                rate[2, c, inner, :] = -scale * total[2] - q[0] * slope_n[c, inner, :]
            return 0

        lax.fori_loop(0, CG, group, 0)

    def apply(top):
        time_step = (COURANT * CELL_SIZE) / top

        def group(c, best):
            for r in range(8):
                inner, rows = pl.ds(r * 8, 8), pl.ds(TOP + r * 8, 8)
                wet = state[0, c + 1, rows, :] + time_step * rate[0, c, inner, :]
                depth = jnp.maximum(wet - time_step * infil[c, inner, :], 0.0)
                slow = approx_recip(1.0 + time_step * drag_k[c, inner, :])
                east = (state[1, c + 1, rows, :] + time_step * rate[1, c, inner, :]) * slow
                north = (state[2, c + 1, rows, :] + time_step * rate[2, c, inner, :]) * slow
                state[0, c + 1, rows, :] = depth
                state[1, c + 1, rows, :] = east
                state[2, c + 1, rows, :] = north
                inverse = approx_recip(jnp.maximum(depth, DEPTH_FLOOR))
                speed = jnp.maximum(jnp.abs(east), jnp.abs(north)) * inverse + root(GRAVITY * depth)
                best = jnp.maximum(best, speed)
            return best

        best = lax.fori_loop(0, CG, group, jnp.zeros((8, 128), F32))
        return jnp.max(best, axis=0, keepdims=True)

    derive_inside()
    for copy in halo_copies(0):
        copy.wait()
    unpack([state.at[0], bed], 0)

    def slopes(c, _):
        for r in range(8):
            inner, rows = pl.ds(r * 8, 8), pl.ds(TOP + r * 8, 8)
            scale = GRAVITY / (2.0 * CELL_SIZE)
            slope_e[c, inner, :] = scale * (east_of(bed, c, rows) - west_of(bed, c, rows))
            slope_n[c, inner, :] = scale * (
                bed[c + 1, pl.ds(TOP + r * 8 + 1, 8), :] - bed[c + 1, pl.ds(TOP + r * 8 - 1, 8), :]
            )
        return 0

    lax.fori_loop(0, CG, slopes, 0)
    derive_edges()
    flux()

    def bulk_wait(buf, s):
        ref = buf.at[pl.ds(0, PEERS)]
        pltpu.make_async_remote_copy(
            src_ref=ref,
            dst_ref=ref,
            send_sem=bulk_sem.at[s],
            recv_sem=bulk_sem.at[s + 1],
            device_id=east_dev,
            device_id_type=LOGICAL,
        ).wait()

    bulk_wait(label_in, 2)

    def label_back(i, _):
        label_tile[pl.ds(i, 1), :] = label_in[i]
        return 0

    lax.fori_loop(0, DEVICES, label_back, 0)
    labels = label_tile[...]
    deep = jnp.max(jnp.max(jnp.where(lanes((DEVICES, 128)) < 16, 0.0, labels), axis=0, keepdims=True), axis=1, keepdims=True)
    top = root(GRAVITY * deep)
    turned = labels.T
    number = turned[0:8] * 16.0 + turned[8:16]
    spots = lax.broadcasted_iota(jnp.int32, (512, 128), 0)
    spots = (lax.rem(spots, TR) * CG + spots // TR).astype(F32)
    for q in range(8):
        label_q[:, pl.ds(q * 128, 128)] = jnp.where(spots == number[q : q + 1, :], 1.0, 0.0).astype(BF16)

    bulk_wait(incoming, 0)
    parts = []
    for q in range(8):
        rows = incoming[:, q, :]
        coarse = rows.astype(BF16)
        parts.append(jnp.concatenate([coarse, (rows - coarse.astype(F32)).astype(BF16)], axis=1))
    both = jnp.dot(label_q[...], jnp.concatenate(parts, axis=0), preferred_element_type=F32)
    severity = (both[:, :128] + both[:, 128:]).reshape(CG, TR, 128)
    infil[...] = infil[...] * jnp.exp(-BURN_LOSS * burn[...].astype(F32) * jnp.maximum(severity, 0.0))
    local = apply(top)

    def step(it, local):
        max_out[it] = local
        for k, o in enumerate(OFFSETS):
            if k == 40:
                pack(state_refs, it)
                for copy in halo_copies(it):
                    copy.start()
            pltpu.make_async_remote_copy(
                src_ref=max_out.at[it],
                dst_ref=max_in.at[it, k],
                send_sem=max_send.at[it],
                recv_sem=max_recv.at[it],
                device_id=target(o),
                device_id_type=LOGICAL,
            ).start()
        derive_inside()
        for copy in halo_copies(it):
            copy.wait()
        unpack(state_refs, it)
        derive_edges()
        flux()
        pltpu.make_async_remote_copy(
            src_ref=max_in.at[it],
            dst_ref=max_in.at[it],
            send_sem=max_send.at[it],
            recv_sem=max_recv.at[it],
            device_id=east_dev,
            device_id_type=LOGICAL,
        ).wait()
        top = jnp.maximum(local, jnp.max(max_in[it], axis=0))
        return apply(jnp.max(top, axis=1, keepdims=True))

    lax.fori_loop(1, ITERS, step, local)

    stores = [
        pltpu.make_async_copy(state.at[f, c + 1, tile_rows], out.at[:, pl.ds(c * 128, 128)], out_sem.at[f, c])
        for f, out in enumerate((depth_out, east_out, north_out))
        for c in range(CG)
    ]
    for copy in stores:
        copy.start()
    for copy in stores:
        copy.wait()


def body(
    reflectance, kernel_id, dest_device, dest_block, regrid_weight, depth0, terrain, rain, burn_mask, land_class,
    infil_table, rough_table,
):
    blocks = reflectance.shape[1]
    grid = jax.ShapeDtypeStruct(depth0.shape, F32)
    cells = (CG, TR, 128)
    padded = (CG + 2, PADR, 128)
    anywhere = pl.BlockSpec(memory_space=pl.ANY)
    scalars = pl.BlockSpec(memory_space=pltpu.SMEM)
    return pl.pallas_call(
        kernel,
        out_shape=(grid, grid, grid),
        in_specs=[anywhere] * 10 + [scalars] * 2,
        out_specs=(anywhere,) * 3,
        scratch_shapes=[
            pltpu.VMEM(reflectance.shape, BF16),
            pltpu.VMEM((1, blocks), jnp.int32),
            pltpu.VMEM((1, blocks), jnp.int32),
            pltpu.VMEM((1, blocks), jnp.int32),
            pltpu.VMEM(regrid_weight.shape, BF16),
            pltpu.VMEM(cells, F32),
            pltpu.VMEM(cells, jnp.int32),
            pltpu.VMEM(cells, jnp.int32),
            pltpu.VMEM((3,) + padded, F32),
            pltpu.VMEM(padded, F32),
            pltpu.VMEM((5,) + padded, F32),
            pltpu.VMEM(cells, F32),
            pltpu.VMEM((3,) + cells, F32),
            pltpu.VMEM(cells, F32),
            pltpu.VMEM(cells, F32),
            pltpu.VMEM(cells, F32),
            pltpu.VMEM(cells, F32),
            pltpu.VMEM((blocks, 128), BF16),
            pltpu.VMEM((DEVICES, 8, 128), F32),
            pltpu.VMEM((DEVICES, 8, 128), F32),
            pltpu.VMEM((DEVICES, 128), F32),
            pltpu.VMEM((DEVICES, 1, 128), F32),
            pltpu.VMEM((DEVICES, 1, 128), F32),
            pltpu.VMEM((512, 1024), BF16),
            pltpu.VMEM((ITERS, 1, 128), F32),
            pltpu.VMEM((ITERS, PEERS, 1, 128), F32),
            pltpu.VMEM((ITERS, 2, 24, 128), F32),
            pltpu.VMEM((ITERS, 2, 24, 128), F32),
            pltpu.VMEM((ITERS, 2, 8, 128), F32),
            pltpu.VMEM((ITERS, 2, 8, 128), F32),
            pltpu.SemaphoreType.DMA((5 + 5 * CG,)),
            pltpu.SemaphoreType.DMA((4,)),
            pltpu.SemaphoreType.DMA((ITERS, 4)),
            pltpu.SemaphoreType.DMA((ITERS, 4)),
            pltpu.SemaphoreType.DMA((ITERS,)),
            pltpu.SemaphoreType.DMA((ITERS,)),
            pltpu.SemaphoreType.DMA((3, CG)),
        ],
        compiler_params=pltpu.CompilerParams(
            collective_id=0, has_side_effects=True, vmem_limit_bytes=48 * 2**20
        ),
        cost_estimate=pl.CostEstimate(flops=10**9, bytes_accessed=3 * 10**6, transcendentals=10**6),
    )(
        reflectance,
        kernel_id.reshape(1, blocks),
        dest_device.reshape(1, blocks),
        dest_block.reshape(1, blocks),
        regrid_weight,
        depth0,
        terrain,
        rain,
        burn_mask,
        land_class,
        infil_table,
        rough_table,
    )


def solution(mesh):
    both = ("row", "col")
    grid = P("row", "col")
    return jax.shard_map(
        body,
        mesh=mesh,
        in_specs=(P(None, both, None), P(both), P(both, None), P(both), P()) + (grid,) * 5 + (P(), P()),
        out_specs=(grid, grid, grid),
        check_vma=False,
    )
```

```python
import jax
import jax.numpy as jnp
from jax import lax
from jax.experimental import pallas as pl
from jax.experimental.pallas import tpu as pltpu
from jax.sharding import PartitionSpec as P

ITERS = 6
GRAVITY = 9.81
CELL_SIZE = 10.0
COURANT = 0.4
DEPTH_FLOOR = 0.05
BURN_LOSS = 1.5
BURN_SMOOTH = 0.5

LOGICAL = pl.DeviceIdType.LOGICAL
F32 = jnp.float32
BF16 = jnp.bfloat16

HOPS = (0, 1, 2, 1)
OFFSETS = sorted(
    [
        (x, core, z, y)
        for x in range(4)
        for core in range(2)
        for z in range(4)
        for y in range(4)
        if (x, core, z, y) != (0, 0, 0, 0)
    ],
    key=lambda o: (-(HOPS[o[0]] + HOPS[o[2]] + HOPS[o[3]]), -o[1]),
)
PEERS = len(OFFSETS)
DEVICES = PEERS + 1

CG = 8
TR = 64
PADR = TR + 16
TOP = 8
GROUPS = 4
GROUP = DEVICES // GROUPS
LINES = 9


def inverse_of(value):
    return pltpu.reciprocal(value, approx=True)


def root(value):
    safe = jnp.maximum(value, 1e-30)
    return safe * lax.rsqrt(safe)


def lanes(shape):
    return lax.broadcasted_iota(jnp.int32, shape, len(shape) - 1)


def nt_dot(a, b):
    return lax.dot_general(a, b, (((1,), (1,)), ((), ())), preferred_element_type=F32)


def kernel(
    refl_hbm, kid_hbm, dest_hbm, block_hbm, weight_hbm, depth_hbm, terrain_hbm, rain_hbm, burn_hbm, land_hbm,
    infil_hbm, rough_hbm,
    state, rate, drag_k, infil, top_out,
    infil_tab, rough_tab, refl, kid, dest, block, weight, rain, burn, land,
    bed, derived, rough2, fade, slope_e, slope_n,
    kid_lines, spread, outgoing, incoming, gathered,
    max_out, max_in, row_out, row_in, col_out, col_in,
    in_sem, bulk_send, bulk_recv, halo_send, halo_recv, max_send, max_recv,
):
    my_row, my_col = lax.axis_index("row"), lax.axis_index("col")
    rows_n, cols_n = 8, 16
    me = my_row * cols_n + my_col
    x, core, z, y = my_row // 2, lax.rem(my_row, 2), my_col // 4, lax.rem(my_col, 4)
    xs = [lax.rem(x + d, 4) * 32 for d in range(4)]
    cores = [lax.rem(core + d, 2) * 16 for d in range(2)]
    zs = [lax.rem(z + d, 4) * 4 for d in range(4)]
    ys = [lax.rem(y + d, 4) for d in range(4)]
    xc = [[a + b for b in cores] for a in xs]
    zy = [[a + b for b in ys] for a in zs]

    def target(o):
        return xc[o[0]][o[1]] + zy[o[2]][o[3]]

    south_dev = lax.rem(my_row + 1, rows_n) * cols_n + my_col
    north_dev = lax.rem(my_row + rows_n - 1, rows_n) * cols_n + my_col
    east_dev = my_row * cols_n + lax.rem(my_col + 1, cols_n)
    west_dev = my_row * cols_n + lax.rem(my_col + cols_n - 1, cols_n)

    def grid_copies(src, dst_of, sem):
        return [
            pltpu.make_async_copy(src.at[:, pl.ds(c * 128, 128)], dst_of(c), sem) for c in range(CG)
        ]

    loads = {
        "dest": [pltpu.make_async_copy(dest_hbm, dest, in_sem.at[0])],
        "kid": [pltpu.make_async_copy(kid_hbm, kid, in_sem.at[1])],
        "block": [pltpu.make_async_copy(block_hbm, block, in_sem.at[2])],
        "refl": [pltpu.make_async_copy(refl_hbm, refl, in_sem.at[3])],
        "weight": [pltpu.make_async_copy(weight_hbm, weight, in_sem.at[4])],
        "tables": [
            pltpu.make_async_copy(infil_hbm, infil_tab, in_sem.at[45]),
            pltpu.make_async_copy(rough_hbm, rough_tab, in_sem.at[46]),
        ],
    }
    tile_rows = pl.ds(TOP, TR)
    grids = {
        "depth": (depth_hbm, lambda c: state.at[0, c + 1, tile_rows], 5),
        "terrain": (terrain_hbm, lambda c: bed.at[c + 1, tile_rows], 6),
        "land": (land_hbm, lambda c: land.at[c], 7),
        "burn": (burn_hbm, lambda c: burn.at[c], 8),
        "rain": (rain_hbm, lambda c: rain.at[c], 9),
    }
    for name, (src, dst_of, slot) in grids.items():
        loads[name] = [
            pltpu.make_async_copy(src.at[:, pl.ds(c * 128, 128)], dst_of(c), in_sem.at[slot + 5 * c])
            for c in range(CG)
        ]
    def begin(*names):
        for name in names:
            for copy in loads[name]:
                copy.start()

    begin("dest", "refl", "block", "kid", "weight")

    def arrive(name):
        for copy in loads[name]:
            copy.wait()

    barrier = pltpu.get_barrier_semaphore()
    for o in OFFSETS:
        pl.semaphore_signal(barrier, inc=1, device_id=target(o), device_id_type=LOGICAL)
    begin("depth", "terrain", "land", "burn", "rain", "tables")

    edge = jnp.zeros((8, 128), F32)
    wide = jnp.zeros((PADR, 128), F32)

    def clear(c, _):
        state[1, c] = wide
        state[2, c] = wide
        for ref in (state.at[0], bed):
            ref[c, pl.ds(0, 8), :] = edge
            ref[c, pl.ds(TOP + TR, 8), :] = edge
        return 0

    lax.fori_loop(0, CG + 2, clear, 0)
    for c in (0, CG + 1):
        state[0, c] = wide
        bed[c] = wide

    arrive("dest")
    arrive("block")
    arrive("kid")
    dest_row = dest[...]
    blocks = dest_row.shape[1]
    member = lax.broadcasted_iota(jnp.int32, (DEVICES, blocks), 0) == dest_row
    member_f = jnp.where(member, 1.0, 0.0).astype(F32)
    member_b = member_f.astype(BF16)
    upper = jnp.where(
        lax.broadcasted_iota(jnp.int32, (blocks, blocks), 0) <= lanes((blocks, blocks)), 1.0, 0.0
    ).astype(BF16)
    counts = jnp.dot(member_b, upper, preferred_element_type=F32)
    rank = jnp.sum(member_f * counts, axis=0, keepdims=True) - 1.0

    block_row = block[...]
    high = (block_row // 16).astype(F32)
    low = lax.rem(block_row, 16).astype(F32)
    line = lax.broadcasted_iota(jnp.int32, (128, blocks), 0)
    by_rank = jnp.where(line.astype(F32) == rank, high, jnp.where(line.astype(F32) - 8.0 == rank, low, 0.0))
    numbers = nt_dot(member_b, by_rank.astype(BF16))

    kid_lines[...] = jnp.broadcast_to(kid[...].astype(F32), (128, blocks)).T
    arrive("refl")

    def index_chunk(i, _):
        rows = pl.ds(pl.multiple_of(i * 64, 64), 64)
        bands = [refl[b, rows, :].astype(F32) for b in range(4)]
        pre = (bands[0] - bands[1]) * inverse_of(bands[0] + bands[1])
        post = (bands[2] - bands[3]) * inverse_of(bands[2] + bands[3])
        index = (pre - post).astype(BF16).astype(F32)
        which = kid_lines[rows, :]
        for k in range(8):
            spread[rows, pl.ds(k * 128, 128)] = jnp.where(which == float(k), index, 0.0).astype(BF16)
        return 0

    lax.fori_loop(0, blocks // 64, index_chunk, 0, unroll=2)
    arrive("weight")
    regridded = jnp.dot(spread[...], weight[...].reshape(8 * 128, 128), preferred_element_type=F32)
    coarse = regridded.astype(BF16)
    halves = jnp.concatenate([coarse, (regridded - coarse.astype(F32)).astype(BF16)], axis=1)

    for q in range(8):
        pick = jnp.where(rank == float(q), member_f, 0.0).astype(BF16)
        both = jnp.dot(pick, halves, preferred_element_type=F32)
        outgoing[:, q, :] = both[:, :128] + both[:, 128:]

    arrive("depth")

    def deepest(c, best):
        return jnp.maximum(best, jnp.max(state[0, c + 1, tile_rows, :].reshape(8, 8, 128), axis=0))

    best = lax.fori_loop(0, CG, deepest, jnp.zeros((8, 128), F32))
    best = jnp.max(jnp.max(best, axis=0, keepdims=True), axis=1, keepdims=True)
    outgoing[:, 8, :] = jnp.where(lanes((DEVICES, 128)) < 16, numbers, best)

    lane_tile = lanes((8, 128))

    def pack(fields, it):
        for f, ref in enumerate(fields):
            for c in range(CG):
                row_out[it, 0, f * CG + c, :] = ref[c + 1, TOP, :]
                row_out[it, 1, f * CG + c, :] = ref[c + 1, TOP + TR - 1, :]
        first = jnp.zeros((8, 128), F32)
        last = jnp.zeros((8, 128), F32)
        for f, ref in enumerate(fields):
            for r in range(8):
                spot = r * 4 + f
                rows = pl.ds(TOP + r * 8, 8)
                first = jnp.where(lane_tile == spot, pltpu.roll(ref[1, rows, :], spot, 1), first)
                last = jnp.where(lane_tile == spot, pltpu.roll(ref[CG, rows, :], spot + 1, 1), last)
        col_out[it, 0] = first
        col_out[it, 1] = last

    def halo_copies(it):
        moves = (
            (row_out, row_in, 0, 1, north_dev, 0),
            (row_out, row_in, 1, 0, south_dev, 1),
            (col_out, col_in, 0, 1, west_dev, 2),
            (col_out, col_in, 1, 0, east_dev, 3),
        )
        return [
            pltpu.make_async_remote_copy(
                src_ref=src.at[it, a],
                dst_ref=dst.at[it, b],
                send_sem=halo_send.at[it, s],
                recv_sem=halo_recv.at[it, s],
                device_id=dev,
                device_id_type=LOGICAL,
            )
            for src, dst, a, b, dev, s in moves
        ]

    keep = (
        jnp.where(my_row > 0, 1.0, 0.0).astype(F32),
        jnp.where(my_row < rows_n - 1, 1.0, 0.0).astype(F32),
        jnp.where(my_col > 0, 1.0, 0.0).astype(F32),
        jnp.where(my_col < cols_n - 1, 1.0, 0.0).astype(F32),
    )

    def unpack(fields, it):
        for f, ref in enumerate(fields):
            for c in range(CG):
                ref[c + 1, TOP - 1, :] = row_in[it, 0, f * CG + c, :] * keep[0]
                ref[c + 1, TOP + TR, :] = row_in[it, 1, f * CG + c, :] * keep[1]
        west = col_in[it, 0] * keep[2]
        east = col_in[it, 1] * keep[3]
        for f, ref in enumerate(fields):
            for r in range(8):
                spot = r * 4 + f
                rows = pl.ds(TOP + r * 8, 8)
                ref[0, rows, :] = pltpu.roll(west, 127 - spot, 1)
                ref[CG + 1, rows, :] = pltpu.roll(east, (128 - spot) % 128, 1)

    state_refs = [state.at[f] for f in range(3)]
    arrive("terrain")
    pack([state.at[0], bed], 0)

    pl.semaphore_wait(barrier, PEERS)

    for copy in halo_copies(0):
        copy.start()
    for k, o in enumerate(OFFSETS):
        there = target(o)
        pltpu.make_async_remote_copy(
            src_ref=outgoing.at[there],
            dst_ref=incoming.at[k],
            send_sem=bulk_send.at[k // GROUP],
            recv_sem=bulk_recv.at[k // GROUP],
            device_id=there,
            device_id_type=LOGICAL,
        ).start()
    incoming[PEERS] = outgoing[me]

    arrive("land")
    arrive("burn")
    arrive("rain")
    arrive("tables")

    def classes(c, _):
        for r in range(8):
            rows = pl.ds(r * 8, 8)
            kind = land[c, rows, :]
            burned = burn[c, rows, :].astype(F32)
            soak = jnp.full((8, 128), infil_tab[0], F32)
            manning = jnp.full((8, 128), rough_tab[0], F32)
            for entry in range(1, 16):
                hit = kind == entry
                soak = jnp.where(hit, infil_tab[entry], soak)
                manning = jnp.where(hit, rough_tab[entry], manning)
            manning = manning * (1.0 - BURN_SMOOTH * burned)
            infil[c, rows, :] = soak
            fade[c, rows, :] = -BURN_LOSS * burned
            rough2[c, rows, :] = GRAVITY * manning * manning
        return 0

    lax.fori_loop(0, CG, classes, 0)

    def west_of(ref, c, rows):
        return pltpu.roll(jnp.where(lane_tile == 127, ref[c, rows, :], ref[c + 1, rows, :]), 1, 1)

    def east_of(ref, c, rows):
        return pltpu.roll(jnp.where(lane_tile == 0, ref[c + 2, rows, :], ref[c + 1, rows, :]), 127, 1)

    def derive(c, rows, r):
        depth, east, north = state[0, c, rows, :], state[1, c, rows, :], state[2, c, rows, :]
        floored = jnp.maximum(depth, DEPTH_FLOOR)
        inverse = inverse_of(floored)
        east_speed, north_speed = east * inverse, north * inverse
        celerity = root(GRAVITY * depth)
        pressure = (0.5 * GRAVITY) * depth * depth
        derived[0, c, rows, :] = east * east_speed + pressure
        derived[1, c, rows, :] = east * north_speed
        derived[2, c, rows, :] = north * north_speed + pressure
        derived[3, c, rows, :] = jnp.abs(east_speed) + celerity
        derived[4, c, rows, :] = jnp.abs(north_speed) + celerity
        if r is not None:
            inner = pl.ds(r * 8, 8)
            magnitude = root(east_speed * east_speed + north_speed * north_speed)
            power = jnp.exp((-4.0 / 3.0) * jnp.log(floored))
            drag_k[c - 1, inner, :] = rough2[c - 1, inner, :] * magnitude * power

    def derive_inside():
        def group(c, _):
            for r in range(8):
                derive(c + 1, pl.ds(TOP + r * 8, 8), r)
            return 0

        lax.fori_loop(0, CG, group, 0)

    def derive_edges():
        def group(c, _):
            derive(c + 1, pl.ds(0, 8), None)
            derive(c + 1, pl.ds(TOP + TR, 8), None)
            return 0

        lax.fori_loop(0, CG, group, 0)
        for c in (0, CG + 1):
            for r in range(8):
                derive(c, pl.ds(TOP + r * 8, 8), None)

    def flux(columns, first, row_groups):
        def group(i, _):
            c = first(i)
            for r in row_groups:
                inner = pl.ds(r * 8, 8)
                rows, above, below = (pl.ds(TOP + r * 8 + s, 8) for s in (0, -1, 1))
                q = [state[f, c + 1, rows, :] for f in range(3)]
                flux_e = [q[1], derived[0, c + 1, rows, :], derived[1, c + 1, rows, :]]
                total = []
                refs = [state.at[0], state.at[1], state.at[2], derived.at[0], derived.at[1], derived.at[3]]
                d_w, e_w, n_w, a_w, b_w, reach_w = [west_of(ref, c, rows) for ref in refs]
                d_e, e_e, n_e, a_e, b_e, reach_e = [east_of(ref, c, rows) for ref in refs]
                reach = derived[3, c + 1, rows, :]
                face_w, face_e = jnp.maximum(reach, reach_w), jnp.maximum(reach, reach_e)
                for mid, q_w, q_e, f_w, f_e in (
                    (q[0], d_w, d_e, e_w, e_e),
                    (q[1], e_w, e_e, a_w, a_e),
                    (q[2], n_w, n_e, b_w, b_e),
                ):
                    total.append((f_e - f_w) - face_e * (q_e - mid) + face_w * (mid - q_w))
                q_n = [state[f, c + 1, above, :] for f in range(3)]
                q_s = [state[f, c + 1, below, :] for f in range(3)]
                reach = derived[4, c + 1, rows, :]
                face_n = jnp.maximum(reach, derived[4, c + 1, above, :])
                face_s = jnp.maximum(reach, derived[4, c + 1, below, :])
                g_n = [q_n[2], derived[1, c + 1, above, :], derived[2, c + 1, above, :]]
                g_s = [q_s[2], derived[1, c + 1, below, :], derived[2, c + 1, below, :]]
                for f in range(3):
                    total[f] = total[f] + (
                        (g_s[f] - g_n[f]) - face_s * (q_s[f] - q[f]) + face_n * (q[f] - q_n[f])
                    )
                scale = 0.5 / CELL_SIZE
                rate[0, c, inner, :] = rain[c, inner, :] - scale * total[0]
                rate[1, c, inner, :] = -scale * total[1] - q[0] * slope_e[c, inner, :]
                rate[2, c, inner, :] = -scale * total[2] - q[0] * slope_n[c, inner, :]
            return 0

        lax.fori_loop(0, columns, group, 0)

    def flux_inside():
        flux(CG - 2, lambda i: i + 1, range(1, 7))

    def flux_edges():
        flux(CG - 2, lambda i: i + 1, (0, 7))
        flux(2, lambda i: i * (CG - 1), range(8))

    def apply(top):
        time_step = (COURANT * CELL_SIZE) / top

        def group(c, best):
            for r in range(8):
                rows = pl.ds(TOP + r * 8, 8)
                depth, east, north = advance(time_step, state, rate, drag_k, infil, c, r)
                state[0, c + 1, rows, :] = depth
                state[1, c + 1, rows, :] = east
                state[2, c + 1, rows, :] = north
                inverse = inverse_of(jnp.maximum(depth, DEPTH_FLOOR))
                speed = jnp.maximum(jnp.abs(east), jnp.abs(north)) * inverse + root(GRAVITY * depth)
                best = jnp.maximum(best, speed)
            return best

        best = lax.fori_loop(0, CG, group, jnp.zeros((8, 128), F32), unroll=4)
        return jnp.max(best, axis=0, keepdims=True)

    for copy in halo_copies(0):
        copy.wait()
    unpack([state.at[0], bed], 0)

    def from_rest(c, _):
        for r in range(8):
            inner = pl.ds(r * 8, 8)
            rows, above, below = (pl.ds(TOP + r * 8 + s, 8) for s in (0, -1, 1))
            gain = GRAVITY / (2.0 * CELL_SIZE)
            tilt_e = gain * (east_of(bed, c, rows) - west_of(bed, c, rows))
            tilt_n = gain * (bed[c + 1, below, :] - bed[c + 1, above, :])
            slope_e[c, inner, :] = tilt_e
            slope_n[c, inner, :] = tilt_n
            mid = state[0, c + 1, rows, :]
            reach = root(GRAVITY * mid)
            scale = 0.5 / CELL_SIZE
            total = 0.0
            rates = []
            for low, high, tilt in (
                (west_of(state.at[0], c, rows), east_of(state.at[0], c, rows), tilt_e),
                (state[0, c + 1, above, :], state[0, c + 1, below, :], tilt_n),
            ):
                face_low = jnp.maximum(reach, root(GRAVITY * low))
                face_high = jnp.maximum(reach, root(GRAVITY * high))
                total = total - face_high * (high - mid) + face_low * (mid - low)
                rates.append((-0.5 * scale * GRAVITY) * (high * high - low * low) - mid * tilt)
            rate[0, c, inner, :] = rain[c, inner, :] - scale * total
            rate[1, c, inner, :] = rates[0]
            rate[2, c, inner, :] = rates[1]
            drag_k[c, inner, :] = jnp.zeros((8, 128), F32)
        return 0

    lax.fori_loop(0, CG, from_rest, 0)

    spots = lax.broadcasted_iota(jnp.int32, (512, 128), 0)
    spots = (lax.rem(spots, TR) * CG + spots // TR).astype(F32)
    sub16, lane16 = lax.broadcasted_iota(jnp.int32, (16, 128), 0), lanes((16, 128))
    join = jnp.where(lane16 == sub16, 16.0, jnp.where(lane16 == sub16 + 8, 1.0, 0.0)).astype(BF16)
    share = 128 // GROUP
    deep = jnp.zeros((GROUP, 128), F32)
    for g in range(GROUPS):
        there = incoming.at[pl.ds(g * GROUP, min(GROUP, PEERS - g * GROUP))]
        pltpu.make_async_remote_copy(
            src_ref=there,
            dst_ref=there,
            send_sem=bulk_send.at[g],
            recv_sem=bulk_recv.at[g],
            device_id=east_dev,
            device_id_type=LOGICAL,
        ).wait()
        sources = pl.ds(g * GROUP, GROUP)
        lines = incoming[sources, 8, :]
        deep = jnp.maximum(deep, jnp.where(lanes((GROUP, 128)) < 16, 0.0, lines))
        number = nt_dot(join, jnp.concatenate([lines.astype(BF16)] * share, axis=0))[:8]
        sub8, lane8 = lax.broadcasted_iota(jnp.int32, (8, 128), 0), lanes((8, 128))
        picks, parts = [], []
        for h in range(8 // share):
            wanted = sub8 == h * share + lane8 // GROUP
            row = jnp.sum(jnp.where(wanted, number, 0.0), axis=0, keepdims=True)
            picks.append(jnp.where(spots == row, 1.0, 0.0).astype(BF16))
        for q in range(8):
            rows = incoming[sources, q, :]
            coarse = rows.astype(BF16)
            parts.append(jnp.concatenate([coarse, (rows - coarse.astype(F32)).astype(BF16)], axis=1))
        part = jnp.dot(jnp.concatenate(picks, axis=1), jnp.concatenate(parts, axis=0), preferred_element_type=F32)
        if g == 0:
            gathered[...] = part
        elif g < GROUPS - 1:
            gathered[...] += part
        else:
            part = part + gathered[...]
    severity = (part[:, :128] + part[:, 128:]).reshape(CG, TR, 128)
    infil[...] = infil[...] * jnp.exp(fade[...] * jnp.maximum(severity, 0.0))
    deep = jnp.max(jnp.max(deep, axis=0, keepdims=True), axis=1, keepdims=True)
    top = root(GRAVITY * deep)
    local = apply(top)

    def before_apply(it, local):
        max_out[it] = local
        for k, o in enumerate(OFFSETS):
            if k == 14:
                pack(state_refs, it)
                for copy in halo_copies(it):
                    copy.start()
            pltpu.make_async_remote_copy(
                src_ref=max_out.at[it],
                dst_ref=max_in.at[it, k],
                send_sem=max_send.at[it],
                recv_sem=max_recv.at[it],
                device_id=target(o),
                device_id_type=LOGICAL,
            ).start()
        derive_inside()
        flux_inside()
        for copy in halo_copies(it):
            copy.wait()
        unpack(state_refs, it)
        derive_edges()
        flux_edges()
        pltpu.make_async_remote_copy(
            src_ref=max_in.at[it],
            dst_ref=max_in.at[it],
            send_sem=max_send.at[it],
            recv_sem=max_recv.at[it],
            device_id=east_dev,
            device_id_type=LOGICAL,
        ).wait()
        top = jnp.maximum(local, jnp.max(max_in[it], axis=0))
        return jnp.max(top, axis=1, keepdims=True)

    def step(it, local):
        return apply(before_apply(it, local))

    local = lax.fori_loop(1, ITERS - 1, step, local)
    top_out[...] = jnp.broadcast_to(before_apply(ITERS - 1, local), (8, 128))


def advance(time_step, state, rate, drag_k, infil, c, r):
    inner, rows = pl.ds(r * 8, 8), pl.ds(TOP + r * 8, 8)
    wet = state[0, c + 1, rows, :] + time_step * rate[0, c, inner, :]
    depth = jnp.maximum(wet - time_step * infil[c, inner, :], 0.0)
    slow = inverse_of(1.0 + time_step * drag_k[c, inner, :])
    east = (state[1, c + 1, rows, :] + time_step * rate[1, c, inner, :]) * slow
    north = (state[2, c + 1, rows, :] + time_step * rate[2, c, inner, :]) * slow
    return depth, east, north


def last_step(state, rate, drag_k, infil, top, depth_out, east_out, north_out, panels, out_sem):
    time_step = (COURANT * CELL_SIZE) / top[...]
    stores = []
    for c in range(CG):
        for r in range(8):
            for f, value in enumerate(advance(time_step, state, rate, drag_k, infil, c, r)):
                panels[f, c, pl.ds(r * 8, 8), :] = value
        for f, out in enumerate((depth_out, east_out, north_out)):
            copy = pltpu.make_async_copy(panels.at[f, c], out.at[:, pl.ds(c * 128, 128)], out_sem.at[f, c])
            copy.start()
            stores.append(copy)
    for copy in stores:
        copy.wait()


def body(
    reflectance, kernel_id, dest_device, dest_block, regrid_weight, depth0, terrain, rain, burn_mask, land_class,
    infil_table, rough_table,
):
    blocks = reflectance.shape[1]
    grid = jax.ShapeDtypeStruct(depth0.shape, F32)
    cells = (CG, TR, 128)
    padded = (CG + 2, PADR, 128)
    anywhere = pl.BlockSpec(memory_space=pl.ANY)
    vmem = pl.BlockSpec(memory_space=pltpu.VMEM)
    operands = (
        reflectance,
        kernel_id.reshape(1, blocks),
        dest_device.reshape(1, blocks),
        dest_block.reshape(1, blocks),
        regrid_weight,
        depth0,
        terrain,
        rain,
        burn_mask,
        land_class,
        infil_table,
        rough_table,
    )
    results = pl.pallas_call(
        kernel,
        out_shape=(
            pltpu.VMEM((3,) + padded, F32),
            pltpu.VMEM((3,) + cells, F32),
            pltpu.VMEM(cells, F32),
            pltpu.VMEM(cells, F32),
            pltpu.VMEM((8, 128), F32),
        ),
        in_specs=[anywhere] * 12,
        out_specs=(vmem,) * 5,
        scratch_shapes=[
            pltpu.SMEM(infil_table.shape, F32),
            pltpu.SMEM(rough_table.shape, F32),
            pltpu.VMEM(reflectance.shape, BF16),
            pltpu.VMEM((1, blocks), jnp.int32),
            pltpu.VMEM((1, blocks), jnp.int32),
            pltpu.VMEM((1, blocks), jnp.int32),
            pltpu.VMEM(regrid_weight.shape, BF16),
            pltpu.VMEM(cells, F32),
            pltpu.VMEM(cells, jnp.int32),
            pltpu.VMEM(cells, jnp.int32),
            pltpu.VMEM(padded, F32),
            pltpu.VMEM((5,) + padded, F32),
            pltpu.VMEM(cells, F32),
            pltpu.VMEM(cells, F32),
            pltpu.VMEM(cells, F32),
            pltpu.VMEM(cells, F32),
            pltpu.VMEM((blocks, 128), F32),
            pltpu.VMEM((blocks, 8 * 128), BF16),
            pltpu.VMEM((DEVICES, LINES, 128), F32),
            pltpu.VMEM((DEVICES, LINES, 128), F32),
            pltpu.VMEM((512, 256), F32),
            pltpu.VMEM((ITERS, 1, 128), F32),
            pltpu.VMEM((ITERS, PEERS, 1, 128), F32),
            pltpu.VMEM((ITERS, 2, 24, 128), F32),
            pltpu.VMEM((ITERS, 2, 24, 128), F32),
            pltpu.VMEM((ITERS, 2, 8, 128), F32),
            pltpu.VMEM((ITERS, 2, 8, 128), F32),
            pltpu.SemaphoreType.DMA((7 + 5 * CG,)),
            pltpu.SemaphoreType.DMA((GROUPS,)),
            pltpu.SemaphoreType.DMA((GROUPS,)),
            pltpu.SemaphoreType.DMA((ITERS, 4)),
            pltpu.SemaphoreType.DMA((ITERS, 4)),
            pltpu.SemaphoreType.DMA((ITERS,)),
            pltpu.SemaphoreType.DMA((ITERS,)),
        ],
        compiler_params=pltpu.CompilerParams(
            collective_id=0, has_side_effects=True, vmem_limit_bytes=48 * 2**20
        ),
        cost_estimate=pl.CostEstimate(flops=10**9, bytes_accessed=3 * 10**6, transcendentals=10**6),
    )(*[pltpu.with_memory_space_constraint(operand, pltpu.HBM) for operand in operands])
    return pl.pallas_call(
        last_step,
        out_shape=(grid, grid, grid),
        in_specs=[vmem] * 5,
        out_specs=(anywhere,) * 3,
        scratch_shapes=[pltpu.VMEM((3,) + cells, F32), pltpu.SemaphoreType.DMA((3, CG))],
        compiler_params=pltpu.CompilerParams(vmem_limit_bytes=4 * 2**20),
    )(*[pltpu.with_memory_space_constraint(result, pltpu.VMEM) for result in results])


def solution(mesh):
    both = ("row", "col")
    grid = P("row", "col")
    return jax.shard_map(
        body,
        mesh=mesh,
        in_specs=(P(None, both, None), P(both), P(both, None), P(both), P()) + (grid,) * 5 + (P(), P()),
        out_specs=(grid, grid, grid),
        check_vma=False,
    )
```

```python
import jax
import jax.numpy as jnp
from jax import lax
from jax.experimental import pallas as pl
from jax.experimental.pallas import tpu as pltpu
from jax.sharding import PartitionSpec as P

ITERS = 6
GRAVITY = 9.81
CELL_SIZE = 10.0
COURANT = 0.4
DEPTH_FLOOR = 0.05
BURN_LOSS = 1.5
BURN_SMOOTH = 0.5

LOGICAL = pl.DeviceIdType.LOGICAL
F32 = jnp.float32
BF16 = jnp.bfloat16

HOPS = (0, 1, 2, 1)
OFFSETS = sorted(
    [
        (x, core, z, y)
        for x in range(4)
        for core in range(2)
        for z in range(4)
        for y in range(4)
        if (x, core, z, y) != (0, 0, 0, 0)
    ],
    key=lambda o: (-(HOPS[o[0]] + HOPS[o[2]] + HOPS[o[3]]), -o[1]),
)
PEERS = len(OFFSETS)
FAR = 14
DEVICES = PEERS + 1

CG = 8
TR = 64
PADR = TR + 16
TOP = 8
GROUPS = (64, 64)
STARTS = [sum(GROUPS[:g]) for g in range(len(GROUPS))]
GROUP_OF = [g for g, size in enumerate(GROUPS) for _ in range(size)]
LINES = 9


def inverse_of(value):
    return pltpu.reciprocal(value, approx=True)


def root(value):
    safe = jnp.maximum(value, 1e-30)
    return safe * lax.rsqrt(safe)


def lanes(shape):
    return lax.broadcasted_iota(jnp.int32, shape, len(shape) - 1)


def nt_dot(a, b):
    return lax.dot_general(a, b, (((1,), (1,)), ((), ())), preferred_element_type=F32)


def kernel(
    refl_hbm, kid_hbm, dest_hbm, block_hbm, weight_hbm, depth_hbm, terrain_hbm, rain_hbm, burn_hbm, land_hbm,
    infil_hbm, rough_hbm,
    state, rate, drag_k, top_out,
    infil, infil_tab, rough_tab, refl, kid, dest, block, weight, rain, burn, land,
    bed, derived, rough2, fade, slope_e, slope_n,
    kid_lines, spread, outgoing, incoming, gathered,
    max_out, max_in, row_out, row_in, col_out, col_in,
    in_sem, bulk_send, bulk_recv, halo_send, halo_recv, max_send, max_recv,
):
    my_row, my_col = lax.axis_index("row"), lax.axis_index("col")
    rows_n, cols_n = 8, 16
    me = my_row * cols_n + my_col
    x, core, z, y = my_row // 2, lax.rem(my_row, 2), my_col // 4, lax.rem(my_col, 4)
    xs = [lax.rem(x + d, 4) * 32 for d in range(4)]
    cores = [lax.rem(core + d, 2) * 16 for d in range(2)]
    zs = [lax.rem(z + d, 4) * 4 for d in range(4)]
    ys = [lax.rem(y + d, 4) for d in range(4)]
    xc = [[a + b for b in cores] for a in xs]
    zy = [[a + b for b in ys] for a in zs]

    def target(o):
        return xc[o[0]][o[1]] + zy[o[2]][o[3]]

    south_dev = lax.rem(my_row + 1, rows_n) * cols_n + my_col
    north_dev = lax.rem(my_row + rows_n - 1, rows_n) * cols_n + my_col
    east_dev = my_row * cols_n + lax.rem(my_col + 1, cols_n)
    west_dev = my_row * cols_n + lax.rem(my_col + cols_n - 1, cols_n)

    def grid_copies(src, dst_of, sem):
        return [
            pltpu.make_async_copy(src.at[:, pl.ds(c * 128, 128)], dst_of(c), sem) for c in range(CG)
        ]

    loads = {
        "dest": [pltpu.make_async_copy(dest_hbm, dest, in_sem.at[0])],
        "kid": [pltpu.make_async_copy(kid_hbm, kid, in_sem.at[1])],
        "block": [pltpu.make_async_copy(block_hbm, block, in_sem.at[2])],
        "refl": [pltpu.make_async_copy(refl_hbm, refl, in_sem.at[3])],
        "weight": [pltpu.make_async_copy(weight_hbm, weight, in_sem.at[4])],
        "tables": [
            pltpu.make_async_copy(infil_hbm, infil_tab, in_sem.at[45]),
            pltpu.make_async_copy(rough_hbm, rough_tab, in_sem.at[46]),
        ],
    }
    tile_rows = pl.ds(TOP, TR)
    grids = {
        "depth": (depth_hbm, lambda c: state.at[0, c + 1, tile_rows], 5),
        "terrain": (terrain_hbm, lambda c: bed.at[c + 1, tile_rows], 6),
        "land": (land_hbm, lambda c: land.at[c], 7),
        "burn": (burn_hbm, lambda c: burn.at[c], 8),
        "rain": (rain_hbm, lambda c: rain.at[c], 9),
    }
    for name, (src, dst_of, slot) in grids.items():
        loads[name] = [
            pltpu.make_async_copy(src.at[:, pl.ds(c * 128, 128)], dst_of(c), in_sem.at[slot + 5 * c])
            for c in range(CG)
        ]
    def begin(*names):
        for name in names:
            for copy in loads[name]:
                copy.start()


    def arrive(name):
        for copy in loads[name]:
            copy.wait()

    barrier = pltpu.get_barrier_semaphore()
    for k, o in enumerate(OFFSETS):
        if k == FAR:
            begin("dest", "refl", "block", "kid", "weight")
        pl.semaphore_signal(barrier, inc=1, device_id=target(o), device_id_type=LOGICAL)
    begin("depth", "terrain", "land", "burn", "rain", "tables")

    edge = jnp.zeros((8, 128), F32)
    wide = jnp.zeros((PADR, 128), F32)

    def clear(c, _):
        state[1, c] = wide
        state[2, c] = wide
        for ref in (state.at[0], bed):
            ref[c, pl.ds(0, 8), :] = edge
            ref[c, pl.ds(TOP + TR, 8), :] = edge
        return 0

    lax.fori_loop(0, CG + 2, clear, 0)
    for c in (0, CG + 1):
        state[0, c] = wide
        bed[c] = wide

    arrive("dest")
    arrive("block")
    arrive("kid")
    dest_row = dest[...]
    blocks = dest_row.shape[1]
    member = lax.broadcasted_iota(jnp.int32, (DEVICES, blocks), 0) == dest_row
    member_f = jnp.where(member, 1.0, 0.0).astype(F32)
    member_b = member_f.astype(BF16)
    upper = jnp.where(
        lax.broadcasted_iota(jnp.int32, (blocks, blocks), 0) <= lanes((blocks, blocks)), 1.0, 0.0
    ).astype(BF16)
    counts = jnp.dot(member_b, upper, preferred_element_type=F32)
    rank = jnp.sum(member_f * counts, axis=0, keepdims=True) - 1.0

    block_row = block[...]
    high = (block_row // 16).astype(F32)
    low = lax.rem(block_row, 16).astype(F32)
    line = lax.broadcasted_iota(jnp.int32, (128, blocks), 0)
    by_rank = jnp.where(line.astype(F32) == rank, high, jnp.where(line.astype(F32) - 8.0 == rank, low, 0.0))
    numbers = nt_dot(member_b, by_rank.astype(BF16))

    kid_lines[...] = jnp.broadcast_to(kid[...].astype(F32), (128, blocks)).T
    arrive("refl")

    def index_chunk(i, _):
        rows = pl.ds(pl.multiple_of(i * 64, 64), 64)
        bands = [refl[b, rows, :].astype(F32) for b in range(4)]
        pre = (bands[0] - bands[1]) * inverse_of(bands[0] + bands[1])
        post = (bands[2] - bands[3]) * inverse_of(bands[2] + bands[3])
        index = (pre - post).astype(BF16).astype(F32)
        which = kid_lines[rows, :]
        for k in range(8):
            spread[rows, pl.ds(k * 128, 128)] = jnp.where(which == float(k), index, 0.0).astype(BF16)
        return 0

    lax.fori_loop(0, blocks // 64, index_chunk, 0, unroll=2)
    arrive("weight")
    regridded = jnp.dot(spread[...], weight[...].reshape(8 * 128, 128), preferred_element_type=F32)
    coarse = regridded.astype(BF16)
    halves = jnp.concatenate([coarse, (regridded - coarse.astype(F32)).astype(BF16)], axis=1)

    for q in range(8):
        pick = jnp.where(rank == float(q), member_f, 0.0).astype(BF16)
        both = jnp.dot(pick, halves, preferred_element_type=F32)
        outgoing[:, q, :] = both[:, :128] + both[:, 128:]

    arrive("depth")

    def deepest(c, best):
        return jnp.maximum(best, jnp.max(state[0, c + 1, tile_rows, :].reshape(8, 8, 128), axis=0))

    best = lax.fori_loop(0, CG, deepest, jnp.zeros((8, 128), F32))
    best = jnp.max(jnp.max(best, axis=0, keepdims=True), axis=1, keepdims=True)
    outgoing[:, 8, :] = jnp.where(lanes((DEVICES, 128)) < 16, numbers, best)

    lane_tile = lanes((8, 128))

    def pack(fields, it):
        for f, ref in enumerate(fields):
            for c in range(CG):
                row_out[it, 0, f * CG + c, :] = ref[c + 1, TOP, :]
                row_out[it, 1, f * CG + c, :] = ref[c + 1, TOP + TR - 1, :]
        first = jnp.zeros((8, 128), F32)
        last = jnp.zeros((8, 128), F32)
        for f, ref in enumerate(fields):
            for r in range(8):
                spot = r * 4 + f
                rows = pl.ds(TOP + r * 8, 8)
                first = jnp.where(lane_tile == spot, pltpu.roll(ref[1, rows, :], spot, 1), first)
                last = jnp.where(lane_tile == spot, pltpu.roll(ref[CG, rows, :], spot + 1, 1), last)
        col_out[it, 0] = first
        col_out[it, 1] = last

    def halo_copies(it):
        moves = (
            (row_out, row_in, 0, 1, north_dev, 0),
            (row_out, row_in, 1, 0, south_dev, 1),
            (col_out, col_in, 0, 1, west_dev, 2),
            (col_out, col_in, 1, 0, east_dev, 3),
        )
        return [
            pltpu.make_async_remote_copy(
                src_ref=src.at[it, a],
                dst_ref=dst.at[it, b],
                send_sem=halo_send.at[it, s],
                recv_sem=halo_recv.at[it, s],
                device_id=dev,
                device_id_type=LOGICAL,
            )
            for src, dst, a, b, dev, s in moves
        ]

    keep = (
        jnp.where(my_row > 0, 1.0, 0.0).astype(F32),
        jnp.where(my_row < rows_n - 1, 1.0, 0.0).astype(F32),
        jnp.where(my_col > 0, 1.0, 0.0).astype(F32),
        jnp.where(my_col < cols_n - 1, 1.0, 0.0).astype(F32),
    )

    def unpack(fields, it):
        for f, ref in enumerate(fields):
            for c in range(CG):
                ref[c + 1, TOP - 1, :] = row_in[it, 0, f * CG + c, :] * keep[0]
                ref[c + 1, TOP + TR, :] = row_in[it, 1, f * CG + c, :] * keep[1]
        west = col_in[it, 0] * keep[2]
        east = col_in[it, 1] * keep[3]
        for f, ref in enumerate(fields):
            for r in range(8):
                spot = r * 4 + f
                rows = pl.ds(TOP + r * 8, 8)
                ref[0, rows, :] = pltpu.roll(west, 127 - spot, 1)
                ref[CG + 1, rows, :] = pltpu.roll(east, (128 - spot) % 128, 1)

    state_refs = [state.at[f] for f in range(3)]
    arrive("terrain")
    pack([state.at[0], bed], 0)

    pl.semaphore_wait(barrier, PEERS)

    for copy in halo_copies(0):
        copy.start()
    for k, o in enumerate(OFFSETS):
        there = target(o)
        pltpu.make_async_remote_copy(
            src_ref=outgoing.at[there],
            dst_ref=incoming.at[k],
            send_sem=bulk_send.at[GROUP_OF[k]],
            recv_sem=bulk_recv.at[GROUP_OF[k]],
            device_id=there,
            device_id_type=LOGICAL,
        ).start()
    incoming[PEERS] = outgoing[me]

    arrive("land")
    arrive("burn")
    arrive("rain")
    arrive("tables")

    def classes(c, _):
        for r in range(8):
            rows = pl.ds(r * 8, 8)
            kind = land[c, rows, :]
            burned = burn[c, rows, :].astype(F32)
            soak = jnp.full((8, 128), infil_tab[0], F32)
            manning = jnp.full((8, 128), rough_tab[0], F32)
            for entry in range(1, 16):
                hit = kind == entry
                soak = jnp.where(hit, infil_tab[entry], soak)
                manning = jnp.where(hit, rough_tab[entry], manning)
            manning = manning * (1.0 - BURN_SMOOTH * burned)
            infil[c, rows, :] = soak
            fade[c, rows, :] = -BURN_LOSS * burned
            rough2[c, rows, :] = GRAVITY * manning * manning
        return 0

    lax.fori_loop(0, CG, classes, 0)

    def west_of(ref, c, rows):
        return pltpu.roll(jnp.where(lane_tile == 127, ref[c, rows, :], ref[c + 1, rows, :]), 1, 1)

    def east_of(ref, c, rows):
        return pltpu.roll(jnp.where(lane_tile == 0, ref[c + 2, rows, :], ref[c + 1, rows, :]), 127, 1)

    def derive(c, rows, r):
        depth, east, north = state[0, c, rows, :], state[1, c, rows, :], state[2, c, rows, :]
        floored = jnp.maximum(depth, DEPTH_FLOOR)
        inverse = inverse_of(floored)
        east_speed, north_speed = east * inverse, north * inverse
        celerity = root(GRAVITY * depth)
        pressure = (0.5 * GRAVITY) * depth * depth
        derived[0, c, rows, :] = east * east_speed + pressure
        derived[1, c, rows, :] = east * north_speed
        derived[2, c, rows, :] = north * north_speed + pressure
        derived[3, c, rows, :] = jnp.abs(east_speed) + celerity
        derived[4, c, rows, :] = jnp.abs(north_speed) + celerity
        if r is not None:
            inner = pl.ds(r * 8, 8)
            magnitude = root(east_speed * east_speed + north_speed * north_speed)
            power = jnp.exp((-4.0 / 3.0) * jnp.log(floored))
            drag_k[c - 1, inner, :] = rough2[c - 1, inner, :] * magnitude * power

    def derive_inside():
        def group(c, _):
            for r in range(8):
                derive(c + 1, pl.ds(TOP + r * 8, 8), r)
            return 0

        lax.fori_loop(0, CG, group, 0)

    def derive_edges():
        def group(c, _):
            derive(c + 1, pl.ds(0, 8), None)
            derive(c + 1, pl.ds(TOP + TR, 8), None)
            return 0

        lax.fori_loop(0, CG, group, 0)
        for c in (0, CG + 1):
            for r in range(8):
                derive(c, pl.ds(TOP + r * 8, 8), None)

    def flux(columns, first, row_groups):
        def group(i, _):
            c = first(i)
            for r in row_groups:
                inner = pl.ds(r * 8, 8)
                rows, above, below = (pl.ds(TOP + r * 8 + s, 8) for s in (0, -1, 1))
                q = [state[f, c + 1, rows, :] for f in range(3)]
                flux_e = [q[1], derived[0, c + 1, rows, :], derived[1, c + 1, rows, :]]
                total = []
                refs = [state.at[0], state.at[1], state.at[2], derived.at[0], derived.at[1], derived.at[3]]
                d_w, e_w, n_w, a_w, b_w, reach_w = [west_of(ref, c, rows) for ref in refs]
                d_e, e_e, n_e, a_e, b_e, reach_e = [east_of(ref, c, rows) for ref in refs]
                reach = derived[3, c + 1, rows, :]
                face_w, face_e = jnp.maximum(reach, reach_w), jnp.maximum(reach, reach_e)
                for mid, q_w, q_e, f_w, f_e in (
                    (q[0], d_w, d_e, e_w, e_e),
                    (q[1], e_w, e_e, a_w, a_e),
                    (q[2], n_w, n_e, b_w, b_e),
                ):
                    total.append((f_e - f_w) - face_e * (q_e - mid) + face_w * (mid - q_w))
                q_n = [state[f, c + 1, above, :] for f in range(3)]
                q_s = [state[f, c + 1, below, :] for f in range(3)]
                reach = derived[4, c + 1, rows, :]
                face_n = jnp.maximum(reach, derived[4, c + 1, above, :])
                face_s = jnp.maximum(reach, derived[4, c + 1, below, :])
                g_n = [q_n[2], derived[1, c + 1, above, :], derived[2, c + 1, above, :]]
                g_s = [q_s[2], derived[1, c + 1, below, :], derived[2, c + 1, below, :]]
                for f in range(3):
                    total[f] = total[f] + (
                        (g_s[f] - g_n[f]) - face_s * (q_s[f] - q[f]) + face_n * (q[f] - q_n[f])
                    )
                scale = 0.5 / CELL_SIZE
                rate[0, c, inner, :] = rain[c, inner, :] - infil[c, inner, :] - scale * total[0]
                rate[1, c, inner, :] = -scale * total[1] - q[0] * slope_e[c, inner, :]
                rate[2, c, inner, :] = -scale * total[2] - q[0] * slope_n[c, inner, :]
            return 0

        lax.fori_loop(0, columns, group, 0)

    def flux_inside():
        flux(CG - 2, lambda i: i + 1, range(1, 7))

    def flux_edges():
        flux(CG - 2, lambda i: i + 1, (0, 7))
        flux(2, lambda i: i * (CG - 1), range(8))

    def apply(top, it):
        time_step = (COURANT * CELL_SIZE) * inverse_of(top)
        best = first = last = jnp.zeros((8, 128), F32)
        for c in range(CG):
            for r in range(8):
                rows = pl.ds(TOP + r * 8, 8)
                values = advance(time_step, state, rate, drag_k, c, r)
                for f, value in enumerate(values):
                    spot = r * 4 + f
                    state[f, c + 1, rows, :] = value
                    if r == 0:
                        row_out[it, 0, f * CG + c, :] = value[0]
                    if r == 7:
                        row_out[it, 1, f * CG + c, :] = value[7]
                    if c == 0:
                        first = jnp.where(lane_tile == spot, pltpu.roll(value, spot, 1), first)
                    if c == CG - 1:
                        last = jnp.where(lane_tile == spot, pltpu.roll(value, spot + 1, 1), last)
                depth, east, north = values
                inverse = inverse_of(jnp.maximum(depth, DEPTH_FLOOR))
                speed = jnp.maximum(jnp.abs(east), jnp.abs(north)) * inverse + root(GRAVITY * depth)
                best = jnp.maximum(best, speed)
        col_out[it, 0] = first
        col_out[it, 1] = last
        return jnp.max(best, axis=0, keepdims=True)

    for copy in halo_copies(0):
        copy.wait_recv()
    unpack([state.at[0], bed], 0)

    def from_rest(c, _):
        for r in range(8):
            inner = pl.ds(r * 8, 8)
            rows, above, below = (pl.ds(TOP + r * 8 + s, 8) for s in (0, -1, 1))
            gain = GRAVITY / (2.0 * CELL_SIZE)
            tilt_e = gain * (east_of(bed, c, rows) - west_of(bed, c, rows))
            tilt_n = gain * (bed[c + 1, below, :] - bed[c + 1, above, :])
            slope_e[c, inner, :] = tilt_e
            slope_n[c, inner, :] = tilt_n
            mid = state[0, c + 1, rows, :]
            reach = root(GRAVITY * mid)
            scale = 0.5 / CELL_SIZE
            total = 0.0
            rates = []
            for low, high, tilt in (
                (west_of(state.at[0], c, rows), east_of(state.at[0], c, rows), tilt_e),
                (state[0, c + 1, above, :], state[0, c + 1, below, :], tilt_n),
            ):
                face_low = jnp.maximum(reach, root(GRAVITY * low))
                face_high = jnp.maximum(reach, root(GRAVITY * high))
                total = total - face_high * (high - mid) + face_low * (mid - low)
                rates.append((-0.5 * scale * GRAVITY) * (high * high - low * low) - mid * tilt)
            rate[0, c, inner, :] = rain[c, inner, :] - scale * total
            rate[1, c, inner, :] = rates[0]
            rate[2, c, inner, :] = rates[1]
            drag_k[c, inner, :] = jnp.zeros((8, 128), F32)
        return 0

    lax.fori_loop(0, CG, from_rest, 0)

    def group_copy(g):
        there = incoming.at[pl.ds(STARTS[g], min(GROUPS[g], PEERS - STARTS[g]))]
        return pltpu.make_async_remote_copy(
            src_ref=there,
            dst_ref=there,
            send_sem=bulk_send.at[g],
            recv_sem=bulk_recv.at[g],
            device_id=east_dev,
            device_id_type=LOGICAL,
        )

    spots = lax.broadcasted_iota(jnp.int32, (512, 128), 0)
    spots = (lax.rem(spots, TR) * CG + spots // TR).astype(F32)
    sub16, lane16 = lax.broadcasted_iota(jnp.int32, (16, 128), 0), lanes((16, 128))
    join = jnp.where(lane16 == sub16, 16.0, jnp.where(lane16 == sub16 + 8, 1.0, 0.0)).astype(BF16)
    deep = jnp.zeros((8, 128), F32)
    for g, size in enumerate(GROUPS):
        group_copy(g).wait_recv()
        sources = pl.ds(STARTS[g], size)
        share = 128 // size
        lines = incoming[sources, 8, :]
        deep = jnp.maximum(deep, jnp.max(lines.reshape(size // 8, 8, 128), axis=0))
        number = nt_dot(join, jnp.concatenate([lines.astype(BF16)] * share, axis=0))[:8]
        sub8, lane8 = lax.broadcasted_iota(jnp.int32, (8, 128), 0), lanes((8, 128))
        picks, parts = [], []
        for h in range(8 // share):
            wanted = sub8 == h * share + lane8 // size
            row = jnp.sum(jnp.where(wanted, number, 0.0), axis=0, keepdims=True)
            picks.append(jnp.where(spots == row, 1.0, 0.0).astype(BF16))
        for q in range(8):
            rows = incoming[sources, q, :]
            coarse = rows.astype(BF16)
            parts.append(jnp.concatenate([coarse, (rows - coarse.astype(F32)).astype(BF16)], axis=1))
        part = jnp.dot(jnp.concatenate(picks, axis=1), jnp.concatenate(parts, axis=0), preferred_element_type=F32)
        if g == 0:
            gathered[...] = part
        elif g < len(GROUPS) - 1:
            gathered[...] += part
        else:
            part = part + gathered[...]
    severity = (part[:, :128] + part[:, 128:]).reshape(CG, TR, 128)
    soaked = infil[...] * jnp.exp(fade[...] * jnp.maximum(severity, 0.0))
    infil[...] = soaked
    rate[0] = rate[0] - soaked
    deep = jnp.where(lanes((8, 128)) < 16, 0.0, deep)
    deep = jnp.max(jnp.max(deep, axis=0, keepdims=True), axis=1, keepdims=True)
    top = root(GRAVITY * deep)
    def max_copy(it, part):
        there = max_in.at[it, pl.ds(*((0, FAR), (FAR, PEERS - FAR))[part])]
        return pltpu.make_async_remote_copy(
            src_ref=there,
            dst_ref=there,
            send_sem=max_send.at[it, part],
            recv_sem=max_recv.at[it, part],
            device_id=east_dev,
            device_id_type=LOGICAL,
        )

    def before_apply(it, local):
        max_out[it] = local
        for k, o in enumerate(OFFSETS):
            if k == FAR:
                for copy in halo_copies(it):
                    copy.start()
            pltpu.make_async_remote_copy(
                src_ref=max_out.at[it],
                dst_ref=max_in.at[it, k],
                send_sem=max_send.at[it, int(k >= FAR)],
                recv_sem=max_recv.at[it, int(k >= FAR)],
                device_id=target(o),
                device_id_type=LOGICAL,
            ).start()
        derive_inside()
        flux_inside()
        for copy in halo_copies(it):
            copy.wait_recv()
        unpack(state_refs, it)
        derive_edges()
        flux_edges()
        max_copy(it, 1).wait_recv()
        top = jnp.maximum(local, jnp.max(max_in[it, pl.ds(FAR, PEERS - FAR)], axis=0))
        max_copy(it, 0).wait_recv()
        top = jnp.maximum(top, jnp.max(max_in[it, pl.ds(0, FAR)], axis=0))
        return jnp.max(top, axis=1, keepdims=True)

    top = lax.fori_loop(1, ITERS, lambda it, top: before_apply(it, apply(top, it)), top)
    top_out[...] = jnp.broadcast_to(top, (8, 128))

    for g in range(len(GROUPS)):
        group_copy(g).wait_send()
    for it in range(ITERS):
        for copy in halo_copies(it):
            copy.wait_send()
        if it > 0:
            max_copy(it, 0).wait_send()
            max_copy(it, 1).wait_send()


def advance(time_step, state, rate, drag_k, c, r):
    inner, rows = pl.ds(r * 8, 8), pl.ds(TOP + r * 8, 8)
    depth = jnp.maximum(state[0, c + 1, rows, :] + time_step * rate[0, c, inner, :], 0.0)
    slow = inverse_of(1.0 + time_step * drag_k[c, inner, :])
    east = (state[1, c + 1, rows, :] + time_step * rate[1, c, inner, :]) * slow
    north = (state[2, c + 1, rows, :] + time_step * rate[2, c, inner, :]) * slow
    return depth, east, north


def last_step(state, rate, drag_k, top, depth_out, east_out, north_out, panels, out_sem):
    time_step = (COURANT * CELL_SIZE) * inverse_of(top[...])
    stores = []
    for r in range(8):
        rows = pl.ds(r * 8, 8)
        for c in range(CG):
            for f, value in enumerate(advance(time_step, state, rate, drag_k, c, r)):
                panels[f, rows, pl.ds(c * 128, 128)] = value
        for f, out in enumerate((depth_out, east_out, north_out)):
            copy = pltpu.make_async_copy(panels.at[f, rows], out.at[rows], out_sem.at[f, r])
            copy.start()
            stores.append(copy)
    for copy in stores:
        copy.wait()


def body(
    reflectance, kernel_id, dest_device, dest_block, regrid_weight, depth0, terrain, rain, burn_mask, land_class,
    infil_table, rough_table,
):
    blocks = reflectance.shape[1]
    grid = jax.ShapeDtypeStruct(depth0.shape, F32)
    cells = (CG, TR, 128)
    padded = (CG + 2, PADR, 128)
    anywhere = pl.BlockSpec(memory_space=pl.ANY)
    vmem = pl.BlockSpec(memory_space=pltpu.VMEM)
    operands = (
        reflectance,
        kernel_id.reshape(1, blocks),
        dest_device.reshape(1, blocks),
        dest_block.reshape(1, blocks),
        regrid_weight,
        depth0,
        terrain,
        rain,
        burn_mask,
        land_class,
        infil_table,
        rough_table,
    )
    results = pl.pallas_call(
        kernel,
        out_shape=(
            pltpu.VMEM((3,) + padded, F32),
            pltpu.VMEM((3,) + cells, F32),
            pltpu.VMEM(cells, F32),
            pltpu.VMEM((8, 128), F32),
        ),
        in_specs=[anywhere] * 12,
        out_specs=(vmem,) * 4,
        scratch_shapes=[
            pltpu.VMEM(cells, F32),
            pltpu.SMEM(infil_table.shape, F32),
            pltpu.SMEM(rough_table.shape, F32),
            pltpu.VMEM(reflectance.shape, BF16),
            pltpu.VMEM((1, blocks), jnp.int32),
            pltpu.VMEM((1, blocks), jnp.int32),
            pltpu.VMEM((1, blocks), jnp.int32),
            pltpu.VMEM(regrid_weight.shape, BF16),
            pltpu.VMEM(cells, F32),
            pltpu.VMEM(cells, jnp.int32),
            pltpu.VMEM(cells, jnp.int32),
            pltpu.VMEM(padded, F32),
            pltpu.VMEM((5,) + padded, F32),
            pltpu.VMEM(cells, F32),
            pltpu.VMEM(cells, F32),
            pltpu.VMEM(cells, F32),
            pltpu.VMEM(cells, F32),
            pltpu.VMEM((blocks, 128), F32),
            pltpu.VMEM((blocks, 8 * 128), BF16),
            pltpu.VMEM((DEVICES, LINES, 128), F32),
            pltpu.VMEM((DEVICES, LINES, 128), F32),
            pltpu.VMEM((512, 256), F32),
            pltpu.VMEM((ITERS, 1, 128), F32),
            pltpu.VMEM((ITERS, PEERS, 1, 128), F32),
            pltpu.VMEM((ITERS, 2, 24, 128), F32),
            pltpu.VMEM((ITERS, 2, 24, 128), F32),
            pltpu.VMEM((ITERS, 2, 8, 128), F32),
            pltpu.VMEM((ITERS, 2, 8, 128), F32),
            pltpu.SemaphoreType.DMA((7 + 5 * CG,)),
            pltpu.SemaphoreType.DMA((len(GROUPS),)),
            pltpu.SemaphoreType.DMA((len(GROUPS),)),
            pltpu.SemaphoreType.DMA((ITERS, 4)),
            pltpu.SemaphoreType.DMA((ITERS, 4)),
            pltpu.SemaphoreType.DMA((ITERS, 2)),
            pltpu.SemaphoreType.DMA((ITERS, 2)),
        ],
        compiler_params=pltpu.CompilerParams(
            collective_id=0, has_side_effects=True, vmem_limit_bytes=48 * 2**20
        ),
        cost_estimate=pl.CostEstimate(flops=10**9, bytes_accessed=3 * 10**6, transcendentals=10**6),
    )(*[pltpu.with_memory_space_constraint(operand, pltpu.HBM) for operand in operands])
    return pl.pallas_call(
        last_step,
        out_shape=(grid, grid, grid),
        in_specs=[vmem] * 4,
        out_specs=(anywhere,) * 3,
        scratch_shapes=[pltpu.VMEM((3,) + depth0.shape, F32), pltpu.SemaphoreType.DMA((3, CG))],
        compiler_params=pltpu.CompilerParams(vmem_limit_bytes=4 * 2**20),
    )(*[pltpu.with_memory_space_constraint(result, pltpu.VMEM) for result in results])


def solution(mesh):
    both = ("row", "col")
    grid = P("row", "col")
    return jax.shard_map(
        body,
        mesh=mesh,
        in_specs=(P(None, both, None), P(both), P(both, None), P(both), P()) + (grid,) * 5 + (P(), P()),
        out_specs=(grid, grid, grid),
        check_vma=False,
    )
```

```python
import jax
import jax.numpy as jnp
from jax import lax
from jax.experimental import pallas as pl
from jax.experimental.pallas import tpu as pltpu
from jax.sharding import PartitionSpec as P

ITERS = 6
GRAVITY = 9.81
CELL_SIZE = 10.0
COURANT = 0.4
DEPTH_FLOOR = 0.05
BURN_LOSS = 1.5
BURN_SMOOTH = 0.5

LOGICAL = pl.DeviceIdType.LOGICAL
F32 = jnp.float32
BF16 = jnp.bfloat16

HOPS = (0, 1, 2, 1)
OFFSETS = sorted(
    [
        (x, core, z, y)
        for x in range(4)
        for core in range(2)
        for z in range(4)
        for y in range(4)
        if (x, core, z, y) != (0, 0, 0, 0)
    ],
    key=lambda o: (-(HOPS[o[0]] + HOPS[o[2]] + HOPS[o[3]]), o[1]),
)
PEERS = len(OFFSETS)
FAR = 14
DEVICES = PEERS + 1

CG = 8
TR = 64
PADR = TR + 16
TOP = 8
GROUPS = (64, 64)
STARTS = [sum(GROUPS[:g]) for g in range(len(GROUPS))]
GROUP_OF = [g for g, size in enumerate(GROUPS) for _ in range(size)]
LINES = 9


def inverse_of(value):
    return pltpu.reciprocal(value, approx=True)


def root(value):
    safe = jnp.maximum(value, 1e-30)
    return safe * lax.rsqrt(safe)


def lanes(shape):
    return lax.broadcasted_iota(jnp.int32, shape, len(shape) - 1)


def nt_dot(a, b):
    return lax.dot_general(a, b, (((1,), (1,)), ((), ())), preferred_element_type=F32)


def kernel(
    refl_hbm, kid_hbm, dest_hbm, block_hbm, weight_hbm, depth_hbm, terrain_hbm, rain_hbm, burn_hbm, land_hbm,
    infil_hbm, rough_hbm,
    state, rate, drag_k, top_out,
    infil, infil_tab, rough_tab, refl, kid, dest, block, weight, rain, burn, land,
    bed, derived, rough2, fade, slope_e, slope_n,
    kid_lines, spread, outgoing, incoming, gathered,
    max_out, max_in, row_out, row_in, col_out, col_in,
    in_sem, bulk_send, bulk_recv, halo_send, halo_recv, max_send, max_recv,
):
    my_row, my_col = lax.axis_index("row"), lax.axis_index("col")
    rows_n, cols_n = 8, 16
    me = my_row * cols_n + my_col
    x, core, z, y = my_row // 2, lax.rem(my_row, 2), my_col // 4, lax.rem(my_col, 4)
    xs = [lax.rem(x + d, 4) * 32 for d in range(4)]
    cores = [lax.rem(core + d, 2) * 16 for d in range(2)]
    zs = [lax.rem(z + d, 4) * 4 for d in range(4)]
    ys = [lax.rem(y + d, 4) for d in range(4)]
    xc = [[a + b for b in cores] for a in xs]
    zy = [[a + b for b in ys] for a in zs]

    def target(o):
        return xc[o[0]][o[1]] + zy[o[2]][o[3]]

    south_dev = lax.rem(my_row + 1, rows_n) * cols_n + my_col
    north_dev = lax.rem(my_row + rows_n - 1, rows_n) * cols_n + my_col
    east_dev = my_row * cols_n + lax.rem(my_col + 1, cols_n)
    west_dev = my_row * cols_n + lax.rem(my_col + cols_n - 1, cols_n)

    def grid_copies(src, dst_of, sem):
        return [
            pltpu.make_async_copy(src.at[:, pl.ds(c * 128, 128)], dst_of(c), sem) for c in range(CG)
        ]

    loads = {
        "dest": [pltpu.make_async_copy(dest_hbm, dest, in_sem.at[0])],
        "kid": [pltpu.make_async_copy(kid_hbm, kid, in_sem.at[1])],
        "block": [pltpu.make_async_copy(block_hbm, block, in_sem.at[2])],
        "refl": [pltpu.make_async_copy(refl_hbm, refl, in_sem.at[3])],
        "weight": [pltpu.make_async_copy(weight_hbm, weight, in_sem.at[4])],
        "tables": [
            pltpu.make_async_copy(infil_hbm, infil_tab, in_sem.at[45]),
            pltpu.make_async_copy(rough_hbm, rough_tab, in_sem.at[46]),
        ],
    }
    tile_rows = pl.ds(TOP, TR)
    grids = {
        "depth": (depth_hbm, lambda c: state.at[0, c + 1, tile_rows], 5),
        "terrain": (terrain_hbm, lambda c: bed.at[c + 1, tile_rows], 6),
        "land": (land_hbm, lambda c: land.at[c], 7),
        "burn": (burn_hbm, lambda c: burn.at[c], 8),
        "rain": (rain_hbm, lambda c: rain.at[c], 9),
    }
    for name, (src, dst_of, slot) in grids.items():
        loads[name] = [
            pltpu.make_async_copy(src.at[:, pl.ds(c * 128, 128)], dst_of(c), in_sem.at[slot + 5 * c])
            for c in range(CG)
        ]
    def begin(*names):
        for name in names:
            for copy in loads[name]:
                copy.start()


    def arrive(name):
        for copy in loads[name]:
            copy.wait()

    barrier = pltpu.get_barrier_semaphore()
    for k, o in enumerate(OFFSETS):
        if k == FAR:
            begin("dest", "refl", "block", "kid", "weight")
        pl.semaphore_signal(barrier, inc=1, device_id=target(o), device_id_type=LOGICAL)
    begin("depth", "terrain", "land", "burn", "rain", "tables")

    edge = jnp.zeros((8, 128), F32)
    wide = jnp.zeros((PADR, 128), F32)

    def clear(c, _):
        state[1, c] = wide
        state[2, c] = wide
        for ref in (state.at[0], bed):
            ref[c, pl.ds(0, 8), :] = edge
            ref[c, pl.ds(TOP + TR, 8), :] = edge
        return 0

    lax.fori_loop(0, CG + 2, clear, 0)
    for c in (0, CG + 1):
        state[0, c] = wide
        bed[c] = wide

    arrive("dest")
    arrive("block")
    arrive("kid")
    dest_row = dest[...]
    blocks = dest_row.shape[1]
    member = lax.broadcasted_iota(jnp.int32, (DEVICES, blocks), 0) == dest_row
    member_f = jnp.where(member, 1.0, 0.0).astype(F32)
    member_b = member_f.astype(BF16)
    upper = jnp.where(
        lax.broadcasted_iota(jnp.int32, (blocks, blocks), 0) <= lanes((blocks, blocks)), 1.0, 0.0
    ).astype(BF16)
    counts = jnp.dot(member_b, upper, preferred_element_type=F32)
    rank = jnp.sum(member_f * counts, axis=0, keepdims=True) - 1.0

    block_row = block[...]
    high = (block_row // 16).astype(F32)
    low = lax.rem(block_row, 16).astype(F32)
    line = lax.broadcasted_iota(jnp.int32, (128, blocks), 0)
    by_rank = jnp.where(line.astype(F32) == rank, high, jnp.where(line.astype(F32) - 8.0 == rank, low, 0.0))
    numbers = nt_dot(member_b, by_rank.astype(BF16))

    kid_lines[...] = jnp.broadcast_to(kid[...].astype(F32), (128, blocks)).T
    arrive("refl")

    def index_chunk(i, _):
        rows = pl.ds(pl.multiple_of(i * 64, 64), 64)
        bands = [refl[b, rows, :].astype(F32) for b in range(4)]
        pre = (bands[0] - bands[1]) * inverse_of(bands[0] + bands[1])
        post = (bands[2] - bands[3]) * inverse_of(bands[2] + bands[3])
        index = (pre - post).astype(BF16).astype(F32)
        which = kid_lines[rows, :]
        for k in range(8):
            spread[rows, pl.ds(k * 128, 128)] = jnp.where(which == float(k), index, 0.0).astype(BF16)
        return 0

    lax.fori_loop(0, blocks // 64, index_chunk, 0, unroll=2)
    arrive("weight")
    regridded = jnp.dot(spread[...], weight[...].reshape(8 * 128, 128), preferred_element_type=F32)
    coarse = regridded.astype(BF16)
    halves = jnp.concatenate([coarse, (regridded - coarse.astype(F32)).astype(BF16)], axis=1)

    for q in range(8):
        pick = jnp.where(rank == float(q), member_f, 0.0).astype(BF16)
        both = jnp.dot(pick, halves, preferred_element_type=F32)
        outgoing[:, q, :] = both[:, :128] + both[:, 128:]

    arrive("depth")

    def deepest(c, best):
        return jnp.maximum(best, jnp.max(state[0, c + 1, tile_rows, :].reshape(8, 8, 128), axis=0))

    best = lax.fori_loop(0, CG, deepest, jnp.zeros((8, 128), F32))
    best = jnp.max(jnp.max(best, axis=0, keepdims=True), axis=1, keepdims=True)
    outgoing[:, 8, :] = jnp.where(lanes((DEVICES, 128)) < 16, numbers, best)

    lane_tile = lanes((8, 128))

    def pack(fields, it):
        for f, ref in enumerate(fields):
            for c in range(CG):
                row_out[it, 0, f * CG + c, :] = ref[c + 1, TOP, :]
                row_out[it, 1, f * CG + c, :] = ref[c + 1, TOP + TR - 1, :]
        first = jnp.zeros((8, 128), F32)
        last = jnp.zeros((8, 128), F32)
        for f, ref in enumerate(fields):
            for r in range(8):
                spot = r * 4 + f
                rows = pl.ds(TOP + r * 8, 8)
                first = jnp.where(lane_tile == spot, pltpu.roll(ref[1, rows, :], spot, 1), first)
                last = jnp.where(lane_tile == spot, pltpu.roll(ref[CG, rows, :], spot + 1, 1), last)
        col_out[it, 0] = first
        col_out[it, 1] = last

    def halo_copies(it):
        moves = (
            (row_out, row_in, 0, 1, north_dev, 0),
            (row_out, row_in, 1, 0, south_dev, 1),
            (col_out, col_in, 0, 1, west_dev, 2),
            (col_out, col_in, 1, 0, east_dev, 3),
        )
        return [
            pltpu.make_async_remote_copy(
                src_ref=src.at[it, a],
                dst_ref=dst.at[it, b],
                send_sem=halo_send.at[it, s],
                recv_sem=halo_recv.at[it, s],
                device_id=dev,
                device_id_type=LOGICAL,
            )
            for src, dst, a, b, dev, s in moves
        ]

    keep = (
        jnp.where(my_row > 0, 1.0, 0.0).astype(F32),
        jnp.where(my_row < rows_n - 1, 1.0, 0.0).astype(F32),
        jnp.where(my_col > 0, 1.0, 0.0).astype(F32),
        jnp.where(my_col < cols_n - 1, 1.0, 0.0).astype(F32),
    )

    def unpack(fields, it):
        for f, ref in enumerate(fields):
            for c in range(CG):
                ref[c + 1, TOP - 1, :] = row_in[it, 0, f * CG + c, :] * keep[0]
                ref[c + 1, TOP + TR, :] = row_in[it, 1, f * CG + c, :] * keep[1]
        west = col_in[it, 0] * keep[2]
        east = col_in[it, 1] * keep[3]
        for f, ref in enumerate(fields):
            for r in range(8):
                spot = r * 4 + f
                rows = pl.ds(TOP + r * 8, 8)
                ref[0, rows, :] = pltpu.roll(west, 127 - spot, 1)
                ref[CG + 1, rows, :] = pltpu.roll(east, (128 - spot) % 128, 1)

    state_refs = [state.at[f] for f in range(3)]
    arrive("terrain")
    pack([state.at[0], bed], 0)

    pl.semaphore_wait(barrier, PEERS)

    for k, o in enumerate(OFFSETS):
        there = target(o)
        if k == FAR:
            for copy in halo_copies(0):
                copy.start()
        pltpu.make_async_remote_copy(
            src_ref=outgoing.at[there],
            dst_ref=incoming.at[k],
            send_sem=bulk_send.at[GROUP_OF[k]],
            recv_sem=bulk_recv.at[GROUP_OF[k]],
            device_id=there,
            device_id_type=LOGICAL,
        ).start()
    incoming[PEERS] = outgoing[me]

    arrive("land")
    arrive("burn")
    arrive("rain")
    arrive("tables")

    def classes(c, _):
        for r in range(8):
            rows = pl.ds(r * 8, 8)
            kind = land[c, rows, :]
            burned = burn[c, rows, :].astype(F32)
            soak = jnp.full((8, 128), infil_tab[0], F32)
            manning = jnp.full((8, 128), rough_tab[0], F32)
            for entry in range(1, 16):
                hit = kind == entry
                soak = jnp.where(hit, infil_tab[entry], soak)
                manning = jnp.where(hit, rough_tab[entry], manning)
            manning = manning * (1.0 - BURN_SMOOTH * burned)
            infil[c, rows, :] = soak
            fade[c, rows, :] = -BURN_LOSS * burned
            rough2[c, rows, :] = GRAVITY * manning * manning
        return 0

    lax.fori_loop(0, CG, classes, 0)

    def west_of(ref, c, rows):
        return pltpu.roll(jnp.where(lane_tile == 127, ref[c, rows, :], ref[c + 1, rows, :]), 1, 1)

    def east_of(ref, c, rows):
        return pltpu.roll(jnp.where(lane_tile == 0, ref[c + 2, rows, :], ref[c + 1, rows, :]), 127, 1)

    def derive(c, rows, r):
        depth, east, north = state[0, c, rows, :], state[1, c, rows, :], state[2, c, rows, :]
        floored = jnp.maximum(depth, DEPTH_FLOOR)
        inverse = inverse_of(floored)
        east_speed, north_speed = east * inverse, north * inverse
        celerity = root(GRAVITY * depth)
        pressure = (0.5 * GRAVITY) * depth * depth
        derived[0, c, rows, :] = east * east_speed + pressure
        derived[1, c, rows, :] = east * north_speed
        derived[2, c, rows, :] = north * north_speed + pressure
        derived[3, c, rows, :] = jnp.abs(east_speed) + celerity
        derived[4, c, rows, :] = jnp.abs(north_speed) + celerity
        if r is not None:
            inner = pl.ds(r * 8, 8)
            magnitude = root(east_speed * east_speed + north_speed * north_speed)
            power = jnp.exp((-4.0 / 3.0) * jnp.log(floored))
            drag_k[c - 1, inner, :] = rough2[c - 1, inner, :] * magnitude * power

    def derive_inside():
        def group(c, _):
            for r in range(8):
                derive(c + 1, pl.ds(TOP + r * 8, 8), r)
            return 0

        lax.fori_loop(0, CG, group, 0)

    def derive_edges():
        def group(c, _):
            derive(c + 1, pl.ds(0, 8), None)
            derive(c + 1, pl.ds(TOP + TR, 8), None)
            return 0

        lax.fori_loop(0, CG, group, 0)
        for c in (0, CG + 1):
            for r in range(8):
                derive(c, pl.ds(TOP + r * 8, 8), None)

    def flux(columns, first, row_groups):
        def group(i, _):
            c = first(i)
            for r in row_groups:
                inner = pl.ds(r * 8, 8)
                rows, above, below = (pl.ds(TOP + r * 8 + s, 8) for s in (0, -1, 1))
                q = [state[f, c + 1, rows, :] for f in range(3)]
                flux_e = [q[1], derived[0, c + 1, rows, :], derived[1, c + 1, rows, :]]
                total = []
                refs = [state.at[0], state.at[1], state.at[2], derived.at[0], derived.at[1], derived.at[3]]
                d_w, e_w, n_w, a_w, b_w, reach_w = [west_of(ref, c, rows) for ref in refs]
                d_e, e_e, n_e, a_e, b_e, reach_e = [east_of(ref, c, rows) for ref in refs]
                reach = derived[3, c + 1, rows, :]
                face_w, face_e = jnp.maximum(reach, reach_w), jnp.maximum(reach, reach_e)
                for mid, q_w, q_e, f_w, f_e in (
                    (q[0], d_w, d_e, e_w, e_e),
                    (q[1], e_w, e_e, a_w, a_e),
                    (q[2], n_w, n_e, b_w, b_e),
                ):
                    total.append((f_e - f_w) - face_e * (q_e - mid) + face_w * (mid - q_w))
                q_n = [state[f, c + 1, above, :] for f in range(3)]
                q_s = [state[f, c + 1, below, :] for f in range(3)]
                reach = derived[4, c + 1, rows, :]
                face_n = jnp.maximum(reach, derived[4, c + 1, above, :])
                face_s = jnp.maximum(reach, derived[4, c + 1, below, :])
                g_n = [q_n[2], derived[1, c + 1, above, :], derived[2, c + 1, above, :]]
                g_s = [q_s[2], derived[1, c + 1, below, :], derived[2, c + 1, below, :]]
                for f in range(3):
                    total[f] = total[f] + (
                        (g_s[f] - g_n[f]) - face_s * (q_s[f] - q[f]) + face_n * (q[f] - q_n[f])
                    )
                scale = 0.5 / CELL_SIZE
                rate[0, c, inner, :] = rain[c, inner, :] - infil[c, inner, :] - scale * total[0]
                rate[1, c, inner, :] = -scale * total[1] - q[0] * slope_e[c, inner, :]
                rate[2, c, inner, :] = -scale * total[2] - q[0] * slope_n[c, inner, :]
            return 0

        lax.fori_loop(0, columns, group, 0)

    def flux_inside():
        flux(CG - 2, lambda i: i + 1, range(1, 7))

    def flux_edges():
        flux(CG - 2, lambda i: i + 1, (0, 7))
        flux(2, lambda i: i * (CG - 1), range(8))

    def apply(top, it):
        time_step = (COURANT * CELL_SIZE) * inverse_of(top)
        best = first = last = jnp.zeros((8, 128), F32)
        for c in range(CG):
            for r in range(8):
                rows = pl.ds(TOP + r * 8, 8)
                values = advance(time_step, state, rate, drag_k, c, r)
                for f, value in enumerate(values):
                    spot = r * 4 + f
                    state[f, c + 1, rows, :] = value
                    if r == 0:
                        row_out[it, 0, f * CG + c, :] = value[0]
                    if r == 7:
                        row_out[it, 1, f * CG + c, :] = value[7]
                    if c == 0:
                        first = jnp.where(lane_tile == spot, pltpu.roll(value, spot, 1), first)
                    if c == CG - 1:
                        last = jnp.where(lane_tile == spot, pltpu.roll(value, spot + 1, 1), last)
                depth, east, north = values
                inverse = inverse_of(jnp.maximum(depth, DEPTH_FLOOR))
                speed = jnp.maximum(jnp.abs(east), jnp.abs(north)) * inverse + root(GRAVITY * depth)
                best = jnp.maximum(best, speed)
        col_out[it, 0] = first
        col_out[it, 1] = last
        return jnp.max(best, axis=0, keepdims=True)

    for copy in halo_copies(0):
        copy.wait_recv()
    unpack([state.at[0], bed], 0)

    def from_rest(c, _):
        for r in range(8):
            inner = pl.ds(r * 8, 8)
            rows, above, below = (pl.ds(TOP + r * 8 + s, 8) for s in (0, -1, 1))
            gain = GRAVITY / (2.0 * CELL_SIZE)
            tilt_e = gain * (east_of(bed, c, rows) - west_of(bed, c, rows))
            tilt_n = gain * (bed[c + 1, below, :] - bed[c + 1, above, :])
            slope_e[c, inner, :] = tilt_e
            slope_n[c, inner, :] = tilt_n
            mid = state[0, c + 1, rows, :]
            reach = root(GRAVITY * mid)
            scale = 0.5 / CELL_SIZE
            total = 0.0
            rates = []
            for low, high, tilt in (
                (west_of(state.at[0], c, rows), east_of(state.at[0], c, rows), tilt_e),
                (state[0, c + 1, above, :], state[0, c + 1, below, :], tilt_n),
            ):
                face_low = jnp.maximum(reach, root(GRAVITY * low))
                face_high = jnp.maximum(reach, root(GRAVITY * high))
                total = total - face_high * (high - mid) + face_low * (mid - low)
                rates.append((-0.5 * scale * GRAVITY) * (high * high - low * low) - mid * tilt)
            rate[0, c, inner, :] = rain[c, inner, :] - scale * total
            rate[1, c, inner, :] = rates[0]
            rate[2, c, inner, :] = rates[1]
            drag_k[c, inner, :] = jnp.zeros((8, 128), F32)
        return 0

    lax.fori_loop(0, CG, from_rest, 0)

    def group_copy(g):
        there = incoming.at[pl.ds(STARTS[g], min(GROUPS[g], PEERS - STARTS[g]))]
        return pltpu.make_async_remote_copy(
            src_ref=there,
            dst_ref=there,
            send_sem=bulk_send.at[g],
            recv_sem=bulk_recv.at[g],
            device_id=east_dev,
            device_id_type=LOGICAL,
        )

    spots = lax.broadcasted_iota(jnp.int32, (512, 128), 0)
    spots = (lax.rem(spots, TR) * CG + spots // TR).astype(F32)
    sub16, lane16 = lax.broadcasted_iota(jnp.int32, (16, 128), 0), lanes((16, 128))
    join = jnp.where(lane16 == sub16, 16.0, jnp.where(lane16 == sub16 + 8, 1.0, 0.0)).astype(BF16)
    deep = jnp.zeros((8, 128), F32)
    for g, size in enumerate(GROUPS):
        group_copy(g).wait_recv()
        sources = pl.ds(STARTS[g], size)
        share = 128 // size
        lines = incoming[sources, 8, :]
        deep = jnp.maximum(deep, jnp.max(lines.reshape(size // 8, 8, 128), axis=0))
        number = nt_dot(join, jnp.concatenate([lines.astype(BF16)] * share, axis=0))[:8]
        sub8, lane8 = lax.broadcasted_iota(jnp.int32, (8, 128), 0), lanes((8, 128))
        picks, parts = [], []
        for h in range(8 // share):
            wanted = sub8 == h * share + lane8 // size
            row = jnp.sum(jnp.where(wanted, number, 0.0), axis=0, keepdims=True)
            picks.append(jnp.where(spots == row, 1.0, 0.0).astype(BF16))
        for q in range(8):
            rows = incoming[sources, q, :]
            coarse = rows.astype(BF16)
            parts.append(jnp.concatenate([coarse, (rows - coarse.astype(F32)).astype(BF16)], axis=1))
        part = jnp.dot(jnp.concatenate(picks, axis=1), jnp.concatenate(parts, axis=0), preferred_element_type=F32)
        if g == 0:
            gathered[...] = part
        elif g < len(GROUPS) - 1:
            gathered[...] += part
        else:
            part = part + gathered[...]
    severity = (part[:, :128] + part[:, 128:]).reshape(CG, TR, 128)
    soaked = infil[...] * jnp.exp(fade[...] * jnp.maximum(severity, 0.0))
    infil[...] = soaked
    rate[0] = rate[0] - soaked
    deep = jnp.where(lanes((8, 128)) < 16, 0.0, deep)
    deep = jnp.max(jnp.max(deep, axis=0, keepdims=True), axis=1, keepdims=True)
    top = root(GRAVITY * deep)
    def max_copy(it, part):
        there = max_in.at[it, pl.ds(*((0, FAR), (FAR, PEERS - FAR))[part])]
        return pltpu.make_async_remote_copy(
            src_ref=there,
            dst_ref=there,
            send_sem=max_send.at[it, part],
            recv_sem=max_recv.at[it, part],
            device_id=east_dev,
            device_id_type=LOGICAL,
        )

    def before_apply(it, local):
        max_out[it] = local
        for k, o in enumerate(OFFSETS):
            if k == FAR:
                for copy in halo_copies(it):
                    copy.start()
            pltpu.make_async_remote_copy(
                src_ref=max_out.at[it],
                dst_ref=max_in.at[it, k],
                send_sem=max_send.at[it, int(k >= FAR)],
                recv_sem=max_recv.at[it, int(k >= FAR)],
                device_id=target(o),
                device_id_type=LOGICAL,
            ).start()
        derive_inside()
        flux_inside()
        for copy in halo_copies(it):
            copy.wait_recv()
        unpack(state_refs, it)
        derive_edges()
        flux_edges()
        max_copy(it, 1).wait_recv()
        top = jnp.maximum(local, jnp.max(max_in[it, pl.ds(FAR, PEERS - FAR)], axis=0))
        max_copy(it, 0).wait_recv()
        top = jnp.maximum(top, jnp.max(max_in[it, pl.ds(0, FAR)], axis=0))
        return jnp.max(top, axis=1, keepdims=True)

    top = lax.fori_loop(1, ITERS, lambda it, top: before_apply(it, apply(top, it)), top)
    top_out[...] = jnp.broadcast_to(top, (8, 128))

    for g in range(len(GROUPS)):
        group_copy(g).wait_send()
    for it in range(ITERS):
        for copy in halo_copies(it):
            copy.wait_send()
        if it > 0:
            max_copy(it, 0).wait_send()
            max_copy(it, 1).wait_send()


def advance(time_step, state, rate, drag_k, c, r):
    inner, rows = pl.ds(r * 8, 8), pl.ds(TOP + r * 8, 8)
    depth = jnp.maximum(state[0, c + 1, rows, :] + time_step * rate[0, c, inner, :], 0.0)
    slow = inverse_of(1.0 + time_step * drag_k[c, inner, :])
    east = (state[1, c + 1, rows, :] + time_step * rate[1, c, inner, :]) * slow
    north = (state[2, c + 1, rows, :] + time_step * rate[2, c, inner, :]) * slow
    return depth, east, north


def last_step(state, rate, drag_k, top, depth_out, east_out, north_out, panels, out_sem):
    time_step = (COURANT * CELL_SIZE) * inverse_of(top[...])
    stores = []
    for r in range(8):
        rows = pl.ds(r * 8, 8)
        for c in range(CG):
            for f, value in enumerate(advance(time_step, state, rate, drag_k, c, r)):
                panels[f, rows, pl.ds(c * 128, 128)] = value
        for f, out in enumerate((depth_out, east_out, north_out)):
            copy = pltpu.make_async_copy(panels.at[f, rows], out.at[rows], out_sem.at[f, r])
            copy.start()
            stores.append(copy)
    for copy in stores:
        copy.wait()


def body(
    reflectance, kernel_id, dest_device, dest_block, regrid_weight, depth0, terrain, rain, burn_mask, land_class,
    infil_table, rough_table,
):
    blocks = reflectance.shape[1]
    grid = jax.ShapeDtypeStruct(depth0.shape, F32)
    cells = (CG, TR, 128)
    padded = (CG + 2, PADR, 128)
    anywhere = pl.BlockSpec(memory_space=pl.ANY)
    vmem = pl.BlockSpec(memory_space=pltpu.VMEM)
    operands = (
        reflectance,
        kernel_id.reshape(1, blocks),
        dest_device.reshape(1, blocks),
        dest_block.reshape(1, blocks),
        regrid_weight,
        depth0,
        terrain,
        rain,
        burn_mask,
        land_class,
        infil_table,
        rough_table,
    )
    results = pl.pallas_call(
        kernel,
        out_shape=(
            pltpu.VMEM((3,) + padded, F32),
            pltpu.VMEM((3,) + cells, F32),
            pltpu.VMEM(cells, F32),
            pltpu.VMEM((8, 128), F32),
        ),
        in_specs=[anywhere] * 12,
        out_specs=(vmem,) * 4,
        scratch_shapes=[
            pltpu.VMEM(cells, F32),
            pltpu.SMEM(infil_table.shape, F32),
            pltpu.SMEM(rough_table.shape, F32),
            pltpu.VMEM(reflectance.shape, BF16),
            pltpu.VMEM((1, blocks), jnp.int32),
            pltpu.VMEM((1, blocks), jnp.int32),
            pltpu.VMEM((1, blocks), jnp.int32),
            pltpu.VMEM(regrid_weight.shape, BF16),
            pltpu.VMEM(cells, F32),
            pltpu.VMEM(cells, jnp.int32),
            pltpu.VMEM(cells, jnp.int32),
            pltpu.VMEM(padded, F32),
            pltpu.VMEM((5,) + padded, F32),
            pltpu.VMEM(cells, F32),
            pltpu.VMEM(cells, F32),
            pltpu.VMEM(cells, F32),
            pltpu.VMEM(cells, F32),
            pltpu.VMEM((blocks, 128), F32),
            pltpu.VMEM((blocks, 8 * 128), BF16),
            pltpu.VMEM((DEVICES, LINES, 128), F32),
            pltpu.VMEM((DEVICES, LINES, 128), F32),
            pltpu.VMEM((512, 256), F32),
            pltpu.VMEM((ITERS, 1, 128), F32),
            pltpu.VMEM((ITERS, PEERS, 1, 128), F32),
            pltpu.VMEM((ITERS, 2, 24, 128), F32),
            pltpu.VMEM((ITERS, 2, 24, 128), F32),
            pltpu.VMEM((ITERS, 2, 8, 128), F32),
            pltpu.VMEM((ITERS, 2, 8, 128), F32),
            pltpu.SemaphoreType.DMA((7 + 5 * CG,)),
            pltpu.SemaphoreType.DMA((len(GROUPS),)),
            pltpu.SemaphoreType.DMA((len(GROUPS),)),
            pltpu.SemaphoreType.DMA((ITERS, 4)),
            pltpu.SemaphoreType.DMA((ITERS, 4)),
            pltpu.SemaphoreType.DMA((ITERS, 2)),
            pltpu.SemaphoreType.DMA((ITERS, 2)),
        ],
        compiler_params=pltpu.CompilerParams(
            collective_id=0, has_side_effects=True, vmem_limit_bytes=48 * 2**20
        ),
        cost_estimate=pl.CostEstimate(flops=10**9, bytes_accessed=3 * 10**6, transcendentals=10**6),
    )(*[pltpu.with_memory_space_constraint(operand, pltpu.HBM) for operand in operands])
    return pl.pallas_call(
        last_step,
        out_shape=(grid, grid, grid),
        in_specs=[vmem] * 4,
        out_specs=(anywhere,) * 3,
        scratch_shapes=[pltpu.VMEM((3,) + depth0.shape, F32), pltpu.SemaphoreType.DMA((3, CG))],
        compiler_params=pltpu.CompilerParams(vmem_limit_bytes=4 * 2**20),
    )(*[pltpu.with_memory_space_constraint(result, pltpu.VMEM) for result in results])


def solution(mesh):
    both = ("row", "col")
    grid = P("row", "col")
    return jax.shard_map(
        body,
        mesh=mesh,
        in_specs=(P(None, both, None), P(both), P(both, None), P(both), P()) + (grid,) * 5 + (P(), P()),
        out_specs=(grid, grid, grid),
        check_vma=False,
    )
```
